128 devices in a mesh: tensor: 8 (over y, core), seq: 16 (over x, z).
Axes of the slice: x: 4, y: 4, z: 4, core: 2. Of those that a mesh axis runs over, the one named last changes fastest.
Arguments:
- tap_low: bfloat16 [8192, 4096], P('seq', 'tensor'), may hold values from -6 to 6
- tap_mid: bfloat16 [8192, 4096], P('seq', 'tensor'), may hold values from -6 to 6
- residual_in: bfloat16 [8192, 4096], P('seq', 'tensor'), may hold values from -3 to 3
- ffn_act: bfloat16 [8192, 14336], P('seq', 'tensor'), may hold values from -127 to 127, as said below
- act_scale: float32 [8192], P('seq'), may hold values from 0.0020044593 to 0.03006689
- down_codes: bfloat16 [14336, 4096], P('tensor'), may hold values from -127 to 127, as said below
- down_scale: int32 [4096], replicated, may hold values from 32 to 319
- join_weight: bfloat16 [12288, 4096], P('seq', 'tensor'), may hold values from -0.0546875 to 0.0546875
- join_gain: float32 [4096], P('tensor'), may hold values from 0.1 to 1.9
- grad_out: bfloat16 [8192, 4096], P('seq', 'tensor'), may hold values from -0.06591797 to 0.06591797
Outputs:
- drafted: bfloat16 [8192, 4096], P('seq', 'tensor')
- grad_join: bfloat16 [12288, 4096], P('seq', 'tensor')
The draws below stay inside these ranges and needn't reach their ends.
Inputs may be any that keep to these rules, and one draw needn't show every extreme that they name: `ffn_act`: whole numbers. `down_codes`: whole numbers.
All inputs are finite; a program needn't handle non-finite values.
Results may differ from the reference program's by a relative error of at most 0.019.
Values may be sent and summed in bfloat16 or wider, within the bound.
A program may use at most 128 MiB of HBM per device.

```python
import math
import jax
import jax.numpy as jnp
from jax import lax

D = 4096
FF = 14336
TAPS = 3
TOK_DEV = 512
TOKENS = 8192
N_SEQ = 16


def eight_bit(key, shape):
    codes_drawn = jax.random.randint(key, shape, -127, 128)
    return codes_drawn.astype(jnp.float32).astype(jnp.bfloat16)


def draw_ffn_act(key, part):
    key = jax.random.fold_in(key, 11)
    return eight_bit(key, (TOKENS, FF))


def draw_down_codes(key, part):
    key = jax.random.fold_in(key, 23)
    return eight_bit(key, (FF, D))


def with_ends(values, rng, low, largest):
    longest = values.shape.index(max(values.shape))
    spots = []
    for shift in (0, 1):
        where = [jax.random.randint(jax.random.fold_in(rng, axis), (), 0, length) for axis, length in enumerate(values.shape)]
        where[longest] = (where[longest] + shift) % values.shape[longest]
        spots.append(tuple(where))
    return values.at[spots[0]].set(low).at[spots[1]].set(largest)


def steps_of(own_key, shape, pieces, smallest, high):
    loudness = 1.0
    for axis_at, parts in pieces:
        draws = jax.random.uniform(jax.random.fold_in(jax.random.fold_in(own_key, 6), axis_at), (parts,), jnp.float32, smallest / len(pieces), high / len(pieces))
        loudness = loudness * jnp.repeat(jnp.exp(draws), shape[axis_at] // parts).reshape((-1,) + (1,) * (len(shape) - 1 - axis_at))
    return loudness


def gaussian(own_key, dims, spread, most, cuts=(), kind=jnp.bfloat16):
    entries = jax.random.normal(own_key, dims, jnp.float32) * spread
    if len(cuts) > 0:
        entries = steps_of(own_key, dims, cuts, -0.22, 0.18) * entries
    return jnp.clip(entries, min=-most, max=most).astype(kind)


def setup_inputs(seed: int = 0) -> dict:
    keys = jax.random.split(jax.random.key(seed), 11)
    return {
        "tap_low": gaussian(keys[0], (TOKENS, D), 1.0, 6.0, ((0, 16), (1, 8))),
        "tap_mid": gaussian(keys[1], (TOKENS, D), 1.0, 6.0, ((0, 16), (1, 8))),
        "residual_in": gaussian(keys[2], (TOKENS, D), 0.5, 3.0, ((0, 16), (1, 8))),
        "ffn_act": draw_ffn_act(jax.random.fold_in(keys[10], 71), 0),
        "act_scale": jnp.clip(jnp.exp(math.log(0.03006689) - 2.7080503 * jax.random.uniform(keys[4], (TOKENS,), jnp.float32) ** steps_of(keys[4], (TOKENS,), ((0, 16),), -0.2, 0.2)), 0.0020044593, 0.03006689),
        "down_codes": draw_down_codes(jax.random.fold_in(keys[10], 71), 0),
        "down_scale": with_ends(jax.random.randint(keys[6], (D,), 32, 320), jax.random.fold_in(keys[6], 1), 32, 319).astype(jnp.int32),
        "join_weight": gaussian(keys[7], (TAPS * D, D), (TAPS * D) ** -0.5, 0.0546875, ((0, 16), (1, 8))),
        "join_gain": jnp.clip(1.0 + 0.18 * jax.random.normal(keys[8], (D,), jnp.float32), 0.1, 1.9),
        "grad_out": gaussian(keys[9], (TOKENS, D), (TOKENS ** -0.5), 0.06591797, ((0, 16), (1, 8))),
    }


QUANT_UNIT = 2.0 ** (-19)

def reference(tap_low, tap_mid, residual_in, ffn_act, act_scale, down_codes, down_scale, join_weight, join_gain, grad_out):
    down_sum = jnp.dot(ffn_act, down_codes, preferred_element_type=jnp.float32)
    col_scale = down_scale.astype(jnp.float32) * QUANT_UNIT
    tap_high = (residual_in.astype(jnp.float32) + down_sum * act_scale[:, None] * col_scale[None, :]).astype(jnp.bfloat16)
    tapped = jnp.concatenate([tap_low, tap_mid, tap_high], axis=1)
    joined_sum = jnp.dot(tapped, join_weight, preferred_element_type=jnp.float32)
    inverse_rms = lax.rsqrt(lax.optimization_barrier(jnp.mean(joined_sum * joined_sum, axis=1, keepdims=True)) + 1e-05)
    normed = joined_sum * inverse_rms
    drafted = (normed * join_gain[None, :]).astype(jnp.bfloat16)
    grad_norm = grad_out.astype(jnp.float32) * join_gain[None, :]
    projection = lax.optimization_barrier(jnp.mean(grad_norm * normed, axis=1, keepdims=True))
    grad_joined = (inverse_rms * (grad_norm - normed * projection)).astype(jnp.bfloat16)
    tap_blocks = tapped.reshape(N_SEQ, TOK_DEV, tapped.shape[1])
    grad_blocks = grad_joined.reshape(N_SEQ, TOK_DEV, grad_joined.shape[1])

    def accumulate(running, pair):
        partial_sum = jnp.dot(pair[0].T, pair[1], preferred_element_type=jnp.float32)
        rounded = lax.optimization_barrier(partial_sum.astype(jnp.bfloat16))
        return (running + rounded.astype(jnp.float32), 0)
    start_sum = jnp.zeros((tapped.shape[1], grad_joined.shape[1]), jnp.float32)
    running, _ = lax.scan(accumulate, start_sum, (tap_blocks, grad_blocks))
    return (drafted, running.astype(jnp.bfloat16))
```

```python
import functools

import jax
import jax.numpy as jnp
from jax import lax
from jax.experimental import pallas as pl
from jax.experimental.pallas import tpu as pltpu
from jax.sharding import PartitionSpec as P

D = 4096
QUANT_UNIT = 2.0 ** (-19)
BF = jnp.bfloat16
F32 = jnp.float32
TOK = 512
COL = 512
UNIT = 256
HID = 1792
SLOTS = 4
CHUNKS = 2
CW = COL // CHUNKS
XB = 3 * UNIT
MESH = pl.DeviceIdType.MESH


def dot(a, b):
    return jnp.dot(a, b, preferred_element_type=F32)


def body(
    tap_low, tap_mid, residual, act, act_scale, codes, col_code, weight, gain, grad_out,
    drafted, grad_join,
    act_v, codes_v, col_v, res_v, go_v, taps, wts, acc,
    d_own, d_ps, d_pr, d_hs, d_hr, d_bs, d_br, high_v,
    j_hs, j_hr, j_bs, j_br, j_v, st_s, st_r, drafted_v,
    gt_v, g_own, g_hs, g_hr, g_bs, g_br, f_s,
    l_sem, c_sem,
    t_recv, t_zs, t_ys, t_fs, t_ps,
    w_own, w_as, w_side, w_d2, w_ss, w_fs,
    dp_recv, dp_send, dh_recv, dh_send, db_recv, db_send,
    jh_recv, jh_send, jb_recv, jb_send,
    st_recv, st_send,
    ga_side, ga_d2, ga_ss, ga_fs,
    gh_recv, gh_send, gb_recv, gb_send,
    f_recv, f_send,
):
    s = lax.axis_index("seq")
    t = lax.axis_index("tensor")
    x, z = lax.div(s, 4), lax.rem(s, 4)
    y, c = lax.div(t, 2), lax.rem(t, 2)

    def wrap(v):
        return lax.rem(v + 4, 4)

    def dev(xx, zz, yy, cc):
        return {"tensor": 2 * yy + cc, "seq": 4 * xx + zz}

    partner = dev(x, z, y, 1 - c)
    y_to = (dev(x, z, wrap(y + 1), c), dev(x, z, wrap(y - 1), c))
    z_to = (dev(x, wrap(z + 1), y, c), dev(x, wrap(z - 1), y, c))
    x_to = (dev(wrap(x + 1), z, y, c), dev(wrap(x - 1), z, y, c))

    sent = []

    def remote(src, dst, send_sem, recv_sem, device):
        return pltpu.make_async_remote_copy(
            src_ref=src, dst_ref=dst, send_sem=send_sem, recv_sem=recv_sem,
            device_id=device, device_id_type=MESH,
        )

    def send(src, dst, send_sem, recv_sem, device):
        copy = remote(src, dst, send_sem, recv_sem, device)
        copy.start()
        sent.append(copy)

    def arrived(dst, sem):
        pltpu.make_async_copy(dst, dst, sem).wait()

    def send_or_copy(src, dst, send_sem, recv_sem, device, own):
        copy = remote(src, dst, send_sem, recv_sem, device)

        @pl.when(own)
        def _():
            pltpu.make_async_copy(src, dst, recv_sem).start()

        @pl.when(jnp.logical_not(own))
        def _():
            copy.start()

        return copy, own

    branched = []

    def code_block(i):
        dy = (2, 1, 3, 0)[i // 2]
        cc = 1 - c if i % 2 == 0 else c
        return 2 * wrap(y + dy) + cc

    def code_copy(i):
        cols = pl.ds(pl.multiple_of(code_block(i) * COL, COL), COL)
        return pltpu.make_async_copy(codes.at[:, cols], codes_v.at[i % SLOTS], c_sem.at[i % SLOTS])

    act_copy = pltpu.make_async_copy(act, act_v, l_sem.at[0])
    act_copy.start()
    for i in range(SLOTS):
        code_copy(i).start()
    res_copy = pltpu.make_async_copy(residual, res_v, l_sem.at[1])
    res_copy.start()
    go_copy = pltpu.make_async_copy(grad_out, go_v, l_sem.at[2])
    go_copy.start()
    col_copy = pltpu.make_async_copy(
        col_code.at[:, pl.ds(pl.multiple_of(t * COL, COL), COL)], col_v, l_sem.at[3]
    )
    col_copy.start()

    barrier = pltpu.get_barrier_semaphore()
    greeted = 0
    for r in range(1, 8):
        pl.semaphore_signal(
            barrier, inc=1, device_id={"tensor": lax.rem(t + r, 8), "seq": s}, device_id_type=MESH
        )
        greeted += 1
    for r in range(1, 4):
        for cc in range(2):
            pl.semaphore_signal(
                barrier, inc=1, device_id=dev(x, wrap(z + r), y, cc), device_id_type=MESH
            )
            greeted += 1
    for device in x_to:
        pl.semaphore_signal(barrier, inc=1, device_id=device, device_id_type=MESH)
        greeted += 1
    pl.semaphore_wait(barrier, greeted)

    def piece(a, ys, zs):
        rows = pl.ds(pl.multiple_of(zs * TOK, TOK), TOK)
        cols = pl.ds(pl.multiple_of((4 * a + ys) * UNIT, UNIT), UNIT)
        return taps.at[rows, cols]

    def tap_out(a, src):
        for e in range(2):
            zd = 2 * c + e
            branched.append(
                send_or_copy(
                    src.at[:, pl.ds(e * UNIT, UNIT)], piece(a, y, z), t_zs.at[a, e],
                    t_recv.at[a, y, z], dev(x, zd, y, lax.div(z, 2)), zd == z,
                )
            )

    def tap_share(a, dy, k):
        ys, zs = wrap(y + dy), 2 * c + k
        here = piece(a, ys, zs)
        send(here, here, t_ps.at[a, dy, k], t_recv.at[a, ys, zs], partner)

    def tap_own(a):
        for k in range(2):
            zs = 2 * c + k
            here = piece(a, y, zs)
            arrived(here, t_recv.at[a, y, zs])
            for way in range(2):
                send(here, here, t_ys.at[a, k, way], t_recv.at[a, y, zs], y_to[way])
        for k in range(2):
            tap_share(a, 0, k)

    def tap_sides(a):
        for way in range(2):
            ys, zs = wrap(y + (3, 1)[way]), 2 * c + way
            here = piece(a, ys, zs)
            arrived(here, t_recv.at[a, ys, zs])
            send(here, here, t_fs.at[a, way], t_recv.at[a, ys, zs], y_to[way])
        for way in range(2):
            dy = (3, 1)[way]
            ys, zs = wrap(y + dy), 2 * c + 1 - way
            arrived(piece(a, ys, zs), t_recv.at[a, ys, zs])
            tap_share(a, dy, way)
            tap_share(a, dy, 1 - way)

    def tap_far(a):
        ys = wrap(y + 2)
        for k in range(2):
            zs = 2 * c + k
            arrived(piece(a, ys, zs), t_recv.at[a, ys, zs])
            tap_share(a, 2, k)

    def tap_partner(a, zs):
        for dy in (0, 1, 3, 2):
            ys = wrap(y + dy)
            arrived(piece(a, ys, zs), t_recv.at[a, ys, zs])

    def w_rows(xx, i, half=None):
        if half is None:
            return wts.at[pl.ds(pl.multiple_of((3 * xx + i) * UNIT, UNIT), UNIT)]
        h = UNIT // 2
        return wts.at[pl.ds(pl.multiple_of((3 * xx + i) * UNIT + half * h, h), h)]

    def w_out():
        for e in range(3):
            q = 3 * z + e
            zd, i = lax.rem(q, 4), lax.div(q, 4)
            branched.append(
                send_or_copy(
                    weight.at[pl.ds(e * UNIT, UNIT)], w_rows(x, i), w_as.at[e], w_own.at[i],
                    dev(x, zd, y, c), zd == z,
                )
            )

    def w_sides():
        for i in range(3):
            arrived(w_rows(x, i), w_own.at[i])
            for way in range(2):
                send(w_rows(x, i), w_rows(x, i), w_ss.at[i, way], w_side.at[i, way], x_to[way])

    def w_forward():
        for i in range(3):
            for way in range(2):
                xx = wrap(x + (3, 1)[way])
                arrived(w_rows(xx, i), w_side.at[i, way])
                half = w_rows(xx, i, way)
                send(half, half, w_fs.at[i, way], w_d2.at[i, way], x_to[way])

    def w_far():
        for i in range(3):
            for way in range(2):
                arrived(w_rows(wrap(x + 2), i, way), w_d2.at[i, way])

    tap_out(0, tap_low)
    tap_out(1, tap_mid)
    w_out()

    def down_block(i):
        code_copy(i).wait()
        part = dot(act_v[...], codes_v[i % SLOTS])
        n = i // 2
        if i % 2 == 0:
            d_ps[n] = part.astype(BF)
            send(d_ps.at[n], d_pr.at[n], dp_send.at[n], dp_recv.at[n], partner)
        else:
            d_own[n] = part
        if i + SLOTS < 8:
            code_copy(i + SLOTS).start()

    H = TOK // 2
    act_copy.wait()
    down_block(0)
    down_block(1)
    tap_own(0)
    down_block(2)
    arrived(d_pr.at[0], dp_recv.at[0])
    for way in range(2):
        rows = slice(way * H, way * H + H)
        d_hs[way] = (d_own[0, rows] + d_pr[0, rows].astype(F32)).astype(BF)
        send(d_hs.at[way], d_hr.at[way], dh_send.at[way], dh_recv.at[way], y_to[way])
    down_block(3)
    w_sides()
    down_block(4)
    down_block(5)
    for way in range(2):
        n = 1 + way
        arrived(d_pr.at[n], dp_recv.at[n])
        rows = slice(way * H, way * H + H)
        other = slice((1 - way) * H, (1 - way) * H + H)
        d_bs[way, other] = (d_own[n, other] + d_pr[n, other].astype(F32)).astype(BF)
        arrived(d_hr.at[way], dh_recv.at[way])
        d_bs[way, rows] = (
            d_own[n, rows] + d_pr[n, rows].astype(F32) + d_hr[way].astype(F32)
        ).astype(BF)
        send(d_bs.at[way], d_br.at[way], db_send.at[way], db_recv.at[way], y_to[way])
    down_block(6)
    down_block(7)
    tap_sides(0)
    tap_own(1)
    w_forward()

    arrived(d_pr.at[3], dp_recv.at[3])
    res_copy.wait()
    col_copy.wait()
    col_full = col_v[...].astype(F32) * QUANT_UNIT
    row_full = jnp.broadcast_to(act_scale[...], (128, TOK)).T[:, :1]
    for way in range(2):
        arrived(d_br.at[way], db_recv.at[way])
    down = d_own[3] + d_pr[3].astype(F32) + d_br[0].astype(F32) + d_br[1].astype(F32)
    high_v[...] = (res_v[...].astype(F32) + down * row_full * col_full).astype(BF)
    tap_out(2, high_v)
    tap_far(0)
    tap_sides(1)

    def join_wait(a, zs, k):
        @pl.when(lax.div(zs, 2) != c)
        def _():
            tap_partner(a, zs)

    def join_part(a, zs):
        rows = pl.ds(pl.multiple_of(zs * TOK, TOK), TOK)
        return dot(taps[rows, a * 1024 : (a + 1) * 1024], wts[a * 1024 : (a + 1) * 1024])

    w_far()

    def join_low(k, _):
        zs = wrap(z + k)
        join_wait(0, zs, k)
        acc[pl.ds(pl.multiple_of(zs * TOK, TOK), TOK)] = join_part(0, zs)
        return 0

    lax.fori_loop(0, 4, join_low, 0)
    tap_own(2)
    tap_far(1)

    def join_mid(k, _):
        zs = wrap(z + k)
        join_wait(1, zs, k)
        acc[pl.ds(pl.multiple_of(zs * TOK, TOK), TOK)] += join_part(1, zs)
        return 0

    lax.fori_loop(0, 4, join_mid, 0)
    tap_sides(2)
    tap_far(2)

    def join_high(k):
        zs = wrap(z + k)
        join_wait(2, zs, k)
        return acc[pl.ds(pl.multiple_of(zs * TOK, TOK), TOK)] + join_part(2, zs)

    part = join_high(2).astype(BF)
    for way in range(2):
        j_hs[way] = part[way * H : way * H + H]
        send(j_hs.at[way], j_hr.at[way], jh_send.at[way], jh_recv.at[way], z_to[way])
    for way in range(2):
        rows = slice(way * H, way * H + H)
        other = slice((1 - way) * H, (1 - way) * H + H)
        j_v[...] = join_high((1, 3)[way])
        j_bs[way, other] = j_v[other].astype(BF)
        arrived(j_hr.at[way], jh_recv.at[way])
        j_bs[way, rows] = (j_v[rows] + j_hr[way].astype(F32)).astype(BF)
        send(j_bs.at[way], j_br.at[way], jb_send.at[way], jb_recv.at[way], z_to[way])
    j_v[...] = join_high(0)
    for way in range(2):
        arrived(j_br.at[way], jb_recv.at[way])
    go_copy.wait()

    R = 128

    def sums(i, _):
        rows = pl.ds(pl.multiple_of(i * R, R), R)
        joined = j_v[rows] + j_br[0, rows].astype(F32) + j_br[1, rows].astype(F32)
        j_v[rows] = joined
        grad_norm = go_v[rows].astype(F32) * gain[...]
        lane = lax.broadcasted_iota(jnp.int32, (R, 128), 1)
        squares = jnp.sum(joined * joined, axis=1, keepdims=True)
        inner = jnp.sum(grad_norm * joined, axis=1, keepdims=True)
        both = jnp.where(lane == 0, squares, jnp.where(lane == 1, inner, 0.0))
        st_s[:, rows] = both.T[:8]
        return 0

    lax.fori_loop(0, TOK // R, sums, 0)
    for r in range(1, 8):
        send(
            st_s, st_r.at[r - 1], st_send.at[r - 1], st_recv.at[r - 1],
            {"tensor": lax.rem(t + r, 8), "seq": s},
        )
    for r in range(1, 8):
        arrived(st_r.at[r - 1], st_recv.at[r - 1])

    own_tokens = pl.multiple_of(z * TOK, TOK)

    def norm(i, _):
        rows = pl.ds(pl.multiple_of(i * R, R), R)
        total = st_s[:, rows]
        for r in range(7):
            total = total + st_r[r, :, rows]
        both = jnp.concatenate([total, jnp.zeros((120, R), F32)], axis=0).T
        inverse_rms = lax.rsqrt(both[:, 0:1] / D + 1e-05)
        projection = inverse_rms * both[:, 1:2] / D
        normed = j_v[rows] * inverse_rms
        drafted_v[rows] = (normed * gain[...]).astype(BF)
        grad_norm = go_v[rows].astype(F32) * gain[...]
        grad_joined = inverse_rms * (grad_norm - normed * projection)
        gt_v[:, pl.ds(pl.multiple_of(own_tokens + i * R, R), R)] = grad_joined.T.astype(BF)
        return 0

    lax.fori_loop(0, TOK // R, norm, 0)

    CH = CW // 2

    def g_piece(n, zs, half=None):
        cols = pl.ds(pl.multiple_of(zs * TOK, TOK), TOK)
        if half is None:
            return gt_v.at[pl.ds(n * CW, CW), cols]
        return gt_v.at[pl.ds(n * CW + half * CH, CH), cols]

    for n in range(CHUNKS):
        for way in range(2):
            send(g_piece(n, z), g_piece(n, z), ga_ss.at[n, way], ga_side.at[n, way], z_to[way])
    drafted_copy = pltpu.make_async_copy(drafted_v, drafted, l_sem.at[4])
    drafted_copy.start()

    def g_forward(n):
        for way in range(2):
            zs = wrap(z + (3, 1)[way])
            arrived(g_piece(n, zs), ga_side.at[n, way])
            send(g_piece(n, zs, way), g_piece(n, zs, way), ga_fs.at[n, way], ga_d2.at[n, way], z_to[way])

    def grad_part(n, dx):
        cols = pl.ds(pl.multiple_of(wrap(x + dx) * XB, XB), XB)
        return dot(gt_v[n * CW : n * CW + CW], taps[:, cols])

    def grad_start(n):
        for way in range(2):
            arrived(g_piece(n, wrap(z + 2), way), ga_d2.at[n, way])
        part = grad_part(n, 2).astype(BF)
        for way in range(2):
            g_hs[n, way] = part[way * CH : way * CH + CH]
            send(g_hs.at[n, way], g_hr.at[n, way], gh_send.at[n, way], gh_recv.at[n, way], x_to[way])

    def grad_sides(n):
        for way in range(2):
            part = grad_part(n, (1, 3)[way])
            arrived(g_hr.at[n, way], gh_recv.at[n, way])
            for half in range(2):
                rows = slice(half * CH, half * CH + CH)
                value = part[rows]
                if half == way:
                    value = value + g_hr[n, way].astype(F32)
                g_bs[n, way, rows] = value.astype(BF)
            send(g_bs.at[n, way], g_br.at[n, way], gb_send.at[n, way], gb_recv.at[n, way], x_to[way])
        g_own[n] = grad_part(n, 0)

    def grad_end(n):
        for way in range(2):
            arrived(g_br.at[n, way], gb_recv.at[n, way])
        for i in range(3):
            rows = slice(i * UNIT, i * UNIT + UNIT)
            total = g_own[n, :, rows] + g_br[n, 0, :, rows].astype(F32) + g_br[n, 1, :, rows].astype(F32)
            f_s[n, rows] = total.T.astype(BF)
            q = 4 * i + z
            zd, e = lax.div(q, 3), lax.rem(q, 3)
            dst = grad_join.at[pl.ds(pl.multiple_of(e * UNIT, UNIT), UNIT), pl.ds(n * CW, CW)]
            branched.append(
                send_or_copy(
                    f_s.at[n, pl.ds(i * UNIT, UNIT)], dst, f_send.at[n, i], f_recv.at[n, e],
                    dev(x, zd, y, c), zd == z,
                )
            )

    for n in range(CHUNKS):
        g_forward(n)
    for n in range(CHUNKS):
        grad_start(n)
        grad_sides(n)
    for n in range(CHUNKS):
        grad_end(n)

    for n in range(CHUNKS):
        for e in range(3):
            arrived(grad_join.at[pl.ds(e * UNIT, UNIT), pl.ds(n * CW, CW)], f_recv.at[n, e])
    drafted_copy.wait()
    for copy in sent:
        copy.wait_send()
    for copy, own in branched:

        @pl.when(jnp.logical_not(own))
        def _(copy=copy):
            copy.wait_send()


def on_device(
    tap_low, tap_mid, residual_in, ffn_act, act_scale, down_codes, down_scale,
    join_weight, join_gain, grad_out,
):
    any_ = pl.BlockSpec(memory_space=pl.ANY)
    vmem = pl.BlockSpec(memory_space=pltpu.VMEM)
    V = pltpu.VMEM
    dma = lambda *shape: pltpu.SemaphoreType.DMA(shape)
    half = TOK // 2
    scratch = [
        V((TOK, HID), BF), V((SLOTS, HID, COL), BF), V((1, COL), jnp.int32),
        V((TOK, COL), BF), V((TOK, COL), BF),
        V((4 * TOK, 12 * UNIT), BF), V((12 * UNIT, COL), BF), V((4 * TOK, COL), F32),
        V((4, TOK, COL), F32), V((4, TOK, COL), BF), V((4, TOK, COL), BF),
        V((2, half, COL), BF), V((2, half, COL), BF), V((2, TOK, COL), BF), V((2, TOK, COL), BF),
        V((TOK, COL), BF),
        V((2, half, COL), BF), V((2, half, COL), BF), V((2, TOK, COL), BF), V((2, TOK, COL), BF),
        V((TOK, COL), F32), V((8, TOK), F32), V((7, 8, TOK), F32), V((TOK, COL), BF),
        V((COL, 4 * TOK), BF), V((CHUNKS, CW, XB), F32),
        V((CHUNKS, 2, CW // 2, XB), BF), V((CHUNKS, 2, CW // 2, XB), BF),
        V((CHUNKS, 2, CW, XB), BF), V((CHUNKS, 2, CW, XB), BF),
        V((CHUNKS, XB, CW), BF),
        dma(5), dma(SLOTS),
        dma(3, 4, 4), dma(3, 2), dma(3, 2, 2), dma(3, 2), dma(3, 4, 2),
        dma(3), dma(3), dma(3, 2), dma(3, 2), dma(3, 2), dma(3, 2),
        dma(4), dma(4), dma(2), dma(2), dma(2), dma(2),
        dma(2), dma(2), dma(2), dma(2),
        dma(7), dma(7),
        dma(CHUNKS, 2), dma(CHUNKS, 2), dma(CHUNKS, 2), dma(CHUNKS, 2),
        dma(CHUNKS, 2), dma(CHUNKS, 2), dma(CHUNKS, 2), dma(CHUNKS, 2),
        dma(CHUNKS, 3), dma(CHUNKS, 3),
    ]
    return pl.pallas_call(
        body,
        out_shape=(
            jax.ShapeDtypeStruct((TOK, COL), BF),
            jax.ShapeDtypeStruct((XB, COL), BF),
        ),
        in_specs=[any_, any_, any_, any_, vmem, any_, any_, any_, vmem, any_],
        out_specs=(any_, any_),
        scratch_shapes=scratch,
        compiler_params=pltpu.CompilerParams(
            collective_id=0, has_side_effects=True, vmem_limit_bytes=63 * 1024 * 1024
        ),
        cost_estimate=pl.CostEstimate(
            flops=20_400_000_000, bytes_accessed=30_000_000, transcendentals=0
        ),
        name="tapped_join",
    )(
        tap_low, tap_mid, residual_in, ffn_act, act_scale.reshape(1, TOK), down_codes,
        down_scale.reshape(1, D), join_weight, join_gain.reshape(1, COL), grad_out,
    )


def solution(mesh):
    return jax.shard_map(
        on_device,
        mesh=mesh,
        in_specs=(
            P("seq", "tensor"),
            P("seq", "tensor"),
            P("seq", "tensor"),
            P("seq", "tensor"),
            P("seq"),
            P("tensor", None),
            P(),
            P("seq", "tensor"),
            P("tensor"),
            P("seq", "tensor"),
        ),
        out_specs=(P("seq", "tensor"), P("seq", "tensor")),
        check_vma=False,
    )
```

```python
import jax
import jax.numpy as jnp
from jax import lax
from jax.experimental import pallas as pl
from jax.experimental.pallas import tpu as pltpu
from jax.sharding import PartitionSpec as P

D = 4096
QUANT_UNIT = 2.0 ** (-19)
BF = jnp.bfloat16
F32 = jnp.float32
TOK = 512
HT = TOK // 2
QT = HT // 2
COL = 512
UNIT = 128
HID = 1792
SLOTS = 4
CHUNKS = 2
CW = COL // CHUNKS
CH = CW // 2
XB = 3 * UNIT
KG = 12 * UNIT
MESH = pl.DeviceIdType.MESH


def dot(a, b):
    return jnp.dot(a, b, preferred_element_type=F32)


def body(
    tap_low, tap_mid, residual, act, act_scale, codes, col_code, weight, gain, grad_out,
    drafted, grad_join,
    act_v, codes_v, col_v, res_v, go_v, taps, wts,
    d_own, d_ps, d_pr, d_hs, d_hr, d_bs, d_br, high_v,
    j_hs, j_hr, j_bs, j_br, j_v, st_s, st_r, drafted_v,
    gt_v, g_own, g_hs, g_hr, g_bs, g_br, f_s,
    l_sem, c_sem,
    t_in, t_side, t_far, t_pp, t_zs, t_ys, t_fs, t_ps,
    w_own, w_as, w_side, w_d2, w_ss, w_fs,
    dp_recv, dp_send, dh_recv, dh_send, db_recv, db_send,
    jh_recv, jh_send, jb_recv, jb_send,
    st_recv, st_send,
    ga_side, ga_d2, ga_ss, ga_fs,
    gh_recv, gh_send, gb_recv, gb_send,
    f_recv, f_send,
):
    s = lax.axis_index("seq")
    t = lax.axis_index("tensor")
    x, z = lax.div(s, 4), lax.rem(s, 4)
    y, c = lax.div(t, 2), lax.rem(t, 2)

    def wrap(v):
        return lax.rem(v + 4, 4)

    def dev(xx, zz, yy, cc):
        return {"tensor": 2 * yy + cc, "seq": 4 * xx + zz}

    partner = dev(x, z, y, 1 - c)
    y_to = (dev(x, z, wrap(y + 1), c), dev(x, z, wrap(y - 1), c))
    z_to = (dev(x, wrap(z + 1), y, c), dev(x, wrap(z - 1), y, c))
    x_to = (dev(wrap(x + 1), z, y, c), dev(wrap(x - 1), z, y, c))
    ring, ring_to = (z, x), (z_to, x_to)
    cross, cross_to = (x, z), (x_to, z_to)

    def on_ring(g, r, cc):
        return dev(x, r, y, cc) if g == 0 else dev(r, z, y, cc)

    sent = []
    branched = []

    def remote(src, dst, send_sem, recv_sem, device):
        return pltpu.make_async_remote_copy(
            src_ref=src, dst_ref=dst, send_sem=send_sem, recv_sem=recv_sem,
            device_id=device, device_id_type=MESH,
        )

    def send(src, dst, send_sem, recv_sem, device):
        copy = remote(src, dst, send_sem, recv_sem, device)
        copy.start()
        sent.append(copy)

    def arrived(dst, sem):
        pltpu.make_async_copy(dst, dst, sem).wait()

    def send_or_copy(src, dst, send_sem, recv_sem, device, own):
        copy = remote(src, dst, send_sem, recv_sem, device)

        @pl.when(own)
        def _():
            pltpu.make_async_copy(src, dst, recv_sem).start()

        @pl.when(jnp.logical_not(own))
        def _():
            copy.start()

        branched.append((copy, own))

    def drain():
        while sent:
            sent.pop(0).wait_send()
        while branched:
            copy, own = branched.pop(0)

            @pl.when(jnp.logical_not(own))
            def _(copy=copy):
                copy.wait_send()

    def code_block(i):
        dy = (2, 1, 3, 0)[i // 2]
        cc = 1 - c if i % 2 == 0 else c
        return 2 * wrap(y + dy) + cc

    def code_copy(i):
        cols = pl.ds(pl.multiple_of(code_block(i) * COL, COL), COL)
        return pltpu.make_async_copy(codes.at[:, cols], codes_v.at[i % SLOTS], c_sem.at[i % SLOTS])

    act_copy = pltpu.make_async_copy(act, act_v, l_sem.at[0])
    act_copy.start()
    for i in range(SLOTS):
        code_copy(i).start()
    res_copy = pltpu.make_async_copy(residual, res_v, l_sem.at[1])
    res_copy.start()
    go_copy = pltpu.make_async_copy(grad_out, go_v, l_sem.at[2])
    go_copy.start()
    col_copy = pltpu.make_async_copy(
        col_code.at[:, pl.ds(pl.multiple_of(t * COL, COL), COL)], col_v, l_sem.at[3]
    )
    col_copy.start()

    barrier = pltpu.get_barrier_semaphore()
    greeted = 0

    def greet(device):
        pl.semaphore_signal(barrier, inc=1, device_id=device, device_id_type=MESH)

    for r in range(1, 8):
        greet({"tensor": lax.rem(t + r, 8), "seq": s})
        greeted += 1
    for g in range(2):
        for r in range(1, 4):
            for cc in range(2):
                greet(on_ring(g, wrap(ring[g] + r), cc))
                greeted += 1
    pl.semaphore_wait(barrier, greeted)

    def place(g, a, ys):
        n = 4 * a + ys
        if g == 0:
            return n
        xo = lax.div(n, 3)
        return 4 * lax.rem(n, 3) + wrap(x - xo)

    def slab(g, a, ys, h, first, count):
        rows = pl.ds(pl.multiple_of((4 * h + first) * HT, HT), count * HT)
        cols = pl.ds(pl.multiple_of(place(g, a, ys) * UNIT, UNIT), UNIT)
        return taps.at[g, rows, cols]

    def tap_out(a, h, src):
        n = 4 * a + y
        for g in range(2):
            for e in range(2):
                j = 2 * c + e
                if g == 0:
                    to, pos = j, n
                else:
                    to, pos = lax.rem(j + lax.div(n, 3), 4), 4 * lax.rem(n, 3) + j
                rows = pl.ds(pl.multiple_of((4 * h + ring[g]) * HT, HT), HT)
                cols = pl.ds(pl.multiple_of(pos * UNIT, UNIT), UNIT)
                send_or_copy(
                    src.at[pl.ds(h * HT, HT), pl.ds((2 * e + g) * UNIT, UNIT)],
                    taps.at[g, rows, cols],
                    t_zs.at[g, a, h, e],
                    t_in.at[g, a, h],
                    on_ring(g, to, lax.div(ring[g], 2)),
                    jnp.logical_and(to == ring[g], lax.div(ring[g], 2) == c),
                )

    def tap_share(g, a, h, dy):
        here = slab(g, a, wrap(y + dy), h, 2 * c, 2)
        send(here, here, t_ps.at[g, a, h, dy], t_pp.at[g, h], partner)

    def tap_own(a, h):
        for g in range(2):
            here = slab(g, a, y, h, 2 * c, 2)
            arrived(here, t_in.at[g, a, h])
            for way in range(2):
                send(here, here, t_ys.at[g, a, h, way], t_side.at[g, a, h, way], y_to[way])
            tap_share(g, a, h, 0)

    def tap_sides(a, h):
        for g in range(2):
            for way in range(2):
                dy = (3, 1)[way]
                ys = wrap(y + dy)
                arrived(slab(g, a, ys, h, 2 * c, 2), t_side.at[g, a, h, way])
                part = slab(g, a, ys, h, 2 * c + way, 1)
                send(part, part, t_fs.at[g, a, h, way], t_far.at[g, a, h], y_to[way])
                tap_share(g, a, h, dy)

    def tap_far(a, h):
        for g in range(2):
            arrived(slab(g, a, wrap(y + 2), h, 2 * c, 2), t_far.at[g, a, h])
            tap_share(g, a, h, 2)

    def tap_partner(h):
        for g in range(2):
            rows = pl.ds(pl.multiple_of((4 * h + 2 * (1 - c)) * HT, HT), 2 * HT)
            arrived(taps.at[g, rows], t_pp.at[g, h])

    def w_rows(g, p, i, half=None):
        if half is None:
            return wts.at[g, pl.ds(pl.multiple_of((3 * p + i) * UNIT, UNIT), UNIT)]
        n = UNIT // 2
        return wts.at[g, pl.ds(pl.multiple_of((3 * p + i) * UNIT + half * n, n), n)]

    def w_out():
        for e in range(3):
            for g in range(2):
                q = 3 * z + e
                if g == 0:
                    to, i = lax.rem(q, 4), lax.div(q, 4)
                else:
                    to, i = lax.rem(q + x, 4), e
                send_or_copy(
                    weight.at[pl.ds((2 * e + g) * UNIT, UNIT)], w_rows(g, cross[g], i),
                    w_as.at[g, e], w_own.at[g, i], on_ring(g, to, c), to == ring[g],
                )

    def w_sides():
        for g in range(2):
            for i in range(3):
                here = w_rows(g, cross[g], i)
                arrived(here, w_own.at[g, i])
                for way in range(2):
                    send(here, here, w_ss.at[g, i, way], w_side.at[g, i, way], cross_to[g][way])

    def w_forward():
        for g in range(2):
            for i in range(3):
                for way in range(2):
                    p = wrap(cross[g] + (3, 1)[way])
                    arrived(w_rows(g, p, i), w_side.at[g, i, way])
                    half = w_rows(g, p, i, way)
                    send(half, half, w_fs.at[g, i, way], w_d2.at[g, i], cross_to[g][way])

    def w_far():
        for g in range(2):
            for i in range(3):
                arrived(w_rows(g, wrap(cross[g] + 2), i), w_d2.at[g, i])

    tap_out(0, 0, tap_low)
    tap_out(1, 0, tap_mid)
    w_out()
    tap_out(0, 1, tap_low)
    tap_out(1, 1, tap_mid)

    def down_block(i):
        code_copy(i).wait()
        part = dot(act_v[...], codes_v[i % SLOTS])
        n = i // 2
        if i % 2 == 0:
            d_ps[n] = part.astype(BF)
            send(d_ps.at[n], d_pr.at[n], dp_send.at[n], dp_recv.at[n], partner)
        else:
            d_own[n] = part
        if i + SLOTS < 8:
            code_copy(i + SLOTS).start()

    def down_far(h):
        for way in range(2):
            rows = slice(h * HT + way * QT, h * HT + way * QT + QT)
            d_hs[h, way] = (d_own[0, rows] + d_pr[0, rows].astype(F32)).astype(BF)
            send(d_hs.at[h, way], d_hr.at[h, way], dh_send.at[h, way], dh_recv.at[h, way], y_to[way])

    def down_sides(h):
        for way in range(2):
            n = 1 + way
            arrived(d_hr.at[h, way], dh_recv.at[h, way])
            for half in range(2):
                rows = slice(h * HT + half * QT, h * HT + half * QT + QT)
                value = d_own[n, rows] + d_pr[n, rows].astype(F32)
                if half == way:
                    value = value + d_hr[h, way].astype(F32)
                d_bs[h, way, half * QT : half * QT + QT] = value.astype(BF)
            send(d_bs.at[h, way], d_br.at[h, way], db_send.at[h, way], db_recv.at[h, way], y_to[way])

    def down_end(h):
        for way in range(2):
            arrived(d_br.at[h, way], db_recv.at[h, way])
        rows = slice(h * HT, h * HT + HT)
        row_full = jnp.broadcast_to(act_scale[:, rows], (128, HT)).T[:, :1]
        col_full = col_v[...].astype(F32) * QUANT_UNIT
        down = d_own[3, rows] + d_pr[3, rows].astype(F32)
        down = down + d_br[h, 0].astype(F32) + d_br[h, 1].astype(F32)
        high_v[rows] = (res_v[rows].astype(F32) + down * row_full * col_full).astype(BF)
        tap_out(2, h, high_v)

    def joined_part(g, h, r):
        rows = pl.ds(pl.multiple_of((4 * h + wrap(ring[g] + r)) * HT, HT), HT)
        return dot(taps[g, rows], wts[g])

    def join_start(h):
        for g in range(2):
            part = joined_part(g, h, 2).astype(BF)
            for way in range(2):
                j_hs[g, h, way] = part[way * QT : way * QT + QT]
                send(
                    j_hs.at[g, h, way], j_hr.at[g, h, way], jh_send.at[g, h, way],
                    jh_recv.at[g, h, way], ring_to[g][way],
                )

    def join_sides(h):
        for g in range(2):
            for way in range(2):
                part = joined_part(g, h, (1, 3)[way])
                arrived(j_hr.at[g, h, way], jh_recv.at[g, h, way])
                for half in range(2):
                    rows = slice(half * QT, half * QT + QT)
                    value = part[rows]
                    if half == way:
                        value = value + j_hr[g, h, way].astype(F32)
                    j_bs[g, h, way, rows] = value.astype(BF)
                send(
                    j_bs.at[g, h, way], j_br.at[g, h, way], jb_send.at[g, h, way],
                    jb_recv.at[g, h, way], ring_to[g][way],
                )

    def join_own(h):
        j_v[h * HT : h * HT + HT] = joined_part(0, h, 0) + joined_part(1, h, 0)

    def join_end(h):
        for g in range(2):
            for way in range(2):
                arrived(j_br.at[g, h, way], jb_recv.at[g, h, way])
        for i in range(2):
            own = slice(i * QT, i * QT + QT)
            rows = slice(h * HT + i * QT, h * HT + i * QT + QT)
            joined = j_v[rows]
            for g in range(2):
                for way in range(2):
                    joined = joined + j_br[g, h, way, own].astype(F32)
            j_v[rows] = joined
            grad_norm = go_v[rows].astype(F32) * gain[...]
            lane = lax.broadcasted_iota(jnp.int32, (QT, 128), 1)
            squares = jnp.sum(joined * joined, axis=1, keepdims=True)
            inner = jnp.sum(grad_norm * joined, axis=1, keepdims=True)
            both = jnp.where(lane == 0, squares, jnp.where(lane == 1, inner, 0.0))
            st_s[h, :, own] = both.T[:8]
        for r in range(1, 8):
            send(
                st_s.at[h], st_r.at[h, r - 1], st_send.at[h, r - 1], st_recv.at[h, r - 1],
                {"tensor": lax.rem(t + r, 8), "seq": s},
            )

    def g_piece(g, h, n, r, half=None):
        cols = pl.ds(pl.multiple_of((4 * h + r) * HT, HT), HT)
        if half is None:
            return gt_v.at[g, pl.ds(n * CW, CW), cols]
        return gt_v.at[g, pl.ds(n * CW + half * CH, CH), cols]

    def norm(h):
        for r in range(1, 8):
            arrived(st_r.at[h, r - 1], st_recv.at[h, r - 1])
        for i in range(2):
            own = slice(i * QT, i * QT + QT)
            rows = slice(h * HT + i * QT, h * HT + i * QT + QT)
            total = st_s[h, :, own]
            for r in range(7):
                total = total + st_r[h, r, :, own]
            both = jnp.concatenate([total, jnp.zeros((120, QT), F32)], axis=0).T
            inverse_rms = lax.rsqrt(both[:, 0:1] / D + 1e-05)
            projection = inverse_rms * both[:, 1:2] / D
            normed = j_v[rows] * inverse_rms
            drafted_v[rows] = (normed * gain[...]).astype(BF)
            grad_norm = go_v[rows].astype(F32) * gain[...]
            grad_joined = inverse_rms * (grad_norm - normed * projection)
            turned = grad_joined.T.astype(BF)
            for g in range(2):
                gt_v[g, :, pl.ds(pl.multiple_of((4 * h + ring[g]) * HT + i * QT, QT), QT)] = turned
        for n in range(CHUNKS):
            for g in range(2):
                here = g_piece(g, h, n, ring[g])
                for way in range(2):
                    send(here, here, ga_ss.at[g, h, n, way], ga_side.at[g, h, n, way], ring_to[g][way])

    def g_forward(h, n):
        for g in range(2):
            for way in range(2):
                r = wrap(ring[g] + (3, 1)[way])
                arrived(g_piece(g, h, n, r), ga_side.at[g, h, n, way])
                part = g_piece(g, h, n, r, way)
                send(part, part, ga_fs.at[g, h, n, way], ga_d2.at[g, h, n], ring_to[g][way])

    def grad_part(g, n, p):
        cols = pl.ds(pl.multiple_of(wrap(cross[g] + p) * XB, XB), XB)
        return dot(gt_v[g, n * CW : n * CW + CW], taps[g, :, cols])

    def grad_start(n):
        for g in range(2):
            for h in range(2):
                arrived(g_piece(g, h, n, wrap(ring[g] + 2)), ga_d2.at[g, h, n])
            part = grad_part(g, n, 2).astype(BF)
            for way in range(2):
                g_hs[g, n, way] = part[way * CH : way * CH + CH]
                send(
                    g_hs.at[g, n, way], g_hr.at[g, n, way], gh_send.at[g, n, way],
                    gh_recv.at[g, n, way], cross_to[g][way],
                )

    def grad_sides(n):
        for g in range(2):
            for way in range(2):
                part = grad_part(g, n, (1, 3)[way])
                arrived(g_hr.at[g, n, way], gh_recv.at[g, n, way])
                for half in range(2):
                    rows = slice(half * CH, half * CH + CH)
                    value = part[rows]
                    if half == way:
                        value = value + g_hr[g, n, way].astype(F32)
                    g_bs[g, n, way, rows] = value.astype(BF)
                send(
                    g_bs.at[g, n, way], g_br.at[g, n, way], gb_send.at[g, n, way],
                    gb_recv.at[g, n, way], cross_to[g][way],
                )

    def grad_own(n):
        for g in range(2):
            g_own[g, n] = grad_part(g, n, 0)

    def grad_end(n):
        for g in range(2):
            for way in range(2):
                arrived(g_br.at[g, n, way], gb_recv.at[g, n, way])
            total = g_own[g, n] + g_br[g, n, 0].astype(F32) + g_br[g, n, 1].astype(F32)
            f_s[g, n] = total.T.astype(BF)
            for i in range(3):
                if g == 0:
                    q = 4 * i + z
                    to, e = lax.div(q, 3), lax.rem(q, 3)
                else:
                    to, e = wrap(x + z - i), i
                rows = pl.ds(pl.multiple_of((2 * e + g) * UNIT, UNIT), UNIT)
                send_or_copy(
                    f_s.at[g, n, pl.ds(i * UNIT, UNIT)],
                    grad_join.at[rows, pl.ds(n * CW, CW)],
                    f_send.at[g, n, i], f_recv.at[g, n, e], on_ring(g, to, c), to == ring[g],
                )

    act_copy.wait()
    down_block(0)
    down_block(1)
    tap_own(0, 0)
    down_block(2)
    arrived(d_pr.at[0], dp_recv.at[0])
    down_far(0)
    down_far(1)
    tap_own(1, 0)
    down_block(3)
    w_sides()
    down_block(4)
    down_block(5)
    for n in (1, 2):
        arrived(d_pr.at[n], dp_recv.at[n])
    down_sides(0)
    down_sides(1)
    down_block(6)
    down_block(7)
    tap_own(0, 1)
    tap_sides(0, 0)
    tap_sides(1, 0)
    w_forward()
    arrived(d_pr.at[3], dp_recv.at[3])
    res_copy.wait()
    col_copy.wait()
    down_end(0)
    tap_own(1, 1)
    down_end(1)
    tap_far(0, 0)
    tap_far(1, 0)
    tap_own(2, 0)
    w_far()
    tap_sides(0, 1)
    tap_own(2, 1)
    tap_sides(1, 1)
    tap_sides(2, 0)
    tap_far(2, 0)
    tap_partner(0)
    go_copy.wait()
    join_start(0)
    join_sides(0)
    join_own(0)
    tap_far(0, 1)
    tap_far(1, 1)
    join_end(0)
    tap_sides(2, 1)
    norm(0)
    tap_far(2, 1)
    tap_partner(1)
    join_start(1)
    join_sides(1)
    join_own(1)
    for n in range(CHUNKS):
        g_forward(0, n)
    join_end(1)
    norm(1)
    drafted_copy = pltpu.make_async_copy(drafted_v, drafted, l_sem.at[4])
    drafted_copy.start()
    for n in range(CHUNKS):
        g_forward(1, n)
    for n in range(CHUNKS):
        grad_start(n)
        grad_sides(n)
        grad_own(n)
    for n in range(CHUNKS):
        grad_end(n)

    drain()
    drafted_copy.wait()
    for n in range(CHUNKS):
        for g in range(2):
            for e in range(3):
                rows = pl.ds((2 * e + g) * UNIT, UNIT)
                arrived(grad_join.at[rows, pl.ds(n * CW, CW)], f_recv.at[g, n, e])


def on_device(
    tap_low, tap_mid, residual_in, ffn_act, act_scale, down_codes, down_scale,
    join_weight, join_gain, grad_out,
):
    any_ = pl.BlockSpec(memory_space=pl.ANY)
    vmem = pl.BlockSpec(memory_space=pltpu.VMEM)
    V = pltpu.VMEM
    dma = lambda *shape: pltpu.SemaphoreType.DMA(shape)
    scratch = [
        V((TOK, HID), BF), V((SLOTS, HID, COL), BF), V((1, COL), jnp.int32),
        V((TOK, COL), BF), V((TOK, COL), BF),
        V((2, 4 * TOK, KG), BF), V((2, KG, COL), BF),
        V((4, TOK, COL), F32), V((4, TOK, COL), BF), V((4, TOK, COL), BF),
        V((2, 2, QT, COL), BF), V((2, 2, QT, COL), BF),
        V((2, 2, HT, COL), BF), V((2, 2, HT, COL), BF),
        V((TOK, COL), BF),
        V((2, 2, 2, QT, COL), BF), V((2, 2, 2, QT, COL), BF),
        V((2, 2, 2, HT, COL), BF), V((2, 2, 2, HT, COL), BF),
        V((TOK, COL), F32), V((2, 8, HT), F32), V((2, 7, 8, HT), F32), V((TOK, COL), BF),
        V((2, COL, 4 * TOK), BF), V((2, CHUNKS, CW, XB), F32),
        V((2, CHUNKS, 2, CH, XB), BF), V((2, CHUNKS, 2, CH, XB), BF),
        V((2, CHUNKS, 2, CW, XB), BF), V((2, CHUNKS, 2, CW, XB), BF),
        V((2, CHUNKS, XB, CW), BF),
        dma(5), dma(SLOTS),
        dma(2, 3, 2), dma(2, 3, 2, 2), dma(2, 3, 2), dma(2, 2),
        dma(2, 3, 2, 2), dma(2, 3, 2, 2), dma(2, 3, 2, 2), dma(2, 3, 2, 4),
        dma(2, 3), dma(2, 3), dma(2, 3, 2), dma(2, 3), dma(2, 3, 2), dma(2, 3, 2),
        dma(4), dma(4), dma(2, 2), dma(2, 2), dma(2, 2), dma(2, 2),
        dma(2, 2, 2), dma(2, 2, 2), dma(2, 2, 2), dma(2, 2, 2),
        dma(2, 7), dma(2, 7),
        dma(2, 2, CHUNKS, 2), dma(2, 2, CHUNKS), dma(2, 2, CHUNKS, 2), dma(2, 2, CHUNKS, 2),
        dma(2, CHUNKS, 2), dma(2, CHUNKS, 2), dma(2, CHUNKS, 2), dma(2, CHUNKS, 2),
        dma(2, CHUNKS, 3), dma(2, CHUNKS, 3),
    ]
    return pl.pallas_call(
        body,
        out_shape=(
            jax.ShapeDtypeStruct((TOK, COL), BF),
            jax.ShapeDtypeStruct((2 * XB, COL), BF),
        ),
        in_specs=[any_, any_, any_, any_, vmem, any_, any_, any_, vmem, any_],
        out_specs=(any_, any_),
        scratch_shapes=scratch,
        compiler_params=pltpu.CompilerParams(
            collective_id=0, has_side_effects=True, vmem_limit_bytes=63 * 1024 * 1024
        ),
        cost_estimate=pl.CostEstimate(
            flops=20_400_000_000, bytes_accessed=30_000_000, transcendentals=0
        ),
        name="tapped_join",
    )(
        tap_low, tap_mid, residual_in, ffn_act, act_scale.reshape(1, TOK), down_codes,
        down_scale.reshape(1, D), join_weight, join_gain.reshape(1, COL), grad_out,
    )


def solution(mesh):
    return jax.shard_map(
        on_device,
        mesh=mesh,
        in_specs=(
            P("seq", "tensor"),
            P("seq", "tensor"),
            P("seq", "tensor"),
            P("seq", "tensor"),
            P("seq"),
            P("tensor", None),
            P(),
            P("seq", "tensor"),
            P("tensor"),
            P("seq", "tensor"),
        ),
        out_specs=(P("seq", "tensor"), P("seq", "tensor")),
        check_vma=False,
    )
```

```python
import jax
import jax.numpy as jnp
from jax import lax
from jax.experimental import pallas as pl
from jax.experimental.pallas import tpu as pltpu
from jax.sharding import PartitionSpec as P

D = 4096
QUANT_UNIT = 2.0 ** (-19)
BF = jnp.bfloat16
F32 = jnp.float32
TOK = 512
NQ = 4
QT = TOK // NQ
HT = TOK // 2
FT = HT // 2
COL = 512
UNIT = 128
HID = 1792
SLOTS = 4
CHUNKS = 2
CW = COL // CHUNKS
CH = CW // 2
XB = 3 * UNIT
KG = 12 * UNIT
MESH = pl.DeviceIdType.MESH


def dot(a, b):
    return jnp.dot(a, b, preferred_element_type=F32)


def body(
    tap_low, tap_mid, residual, act, act_scale, codes, col_code, weight, gain, grad_out,
    drafted, grad_join,
    act_v, codes_v, col_v, res_v, go_v, taps, wts,
    d_own, d_ps, d_pr, d_hs, d_hr, d_bs, d_br, high_v,
    j_s, j_r, j_v, st_s, st_r, drafted_v,
    gt_v, g_own, g_hs, g_hr, g_bs, g_br, f_s,
    l_sem, c_sem,
    t_in, t_side, t_far, t_pp, t_zs, t_ys, t_fs, t_ps,
    w_own, w_as, w_side, w_d2, w_ss, w_fs,
    dp_recv, dp_send, dh_recv, dh_send, db_recv, db_send,
    j_recv, j_send, st_recv, st_send, a_recv, a_send,
    gh_recv, gh_send, gb_recv, gb_send,
    f_recv, f_send,
):
    s = lax.axis_index("seq")
    t = lax.axis_index("tensor")
    x, z = lax.div(s, 4), lax.rem(s, 4)
    y, c = lax.div(t, 2), lax.rem(t, 2)

    def wrap(v):
        return lax.rem(v + 4, 4)

    def dev(xx, zz, yy, cc):
        return {"tensor": 2 * yy + cc, "seq": 4 * xx + zz}

    partner = dev(x, z, y, 1 - c)
    y_to = (dev(x, z, wrap(y + 1), c), dev(x, z, wrap(y - 1), c))
    z_to = (dev(x, wrap(z + 1), y, c), dev(x, wrap(z - 1), y, c))
    x_to = (dev(wrap(x + 1), z, y, c), dev(wrap(x - 1), z, y, c))
    ring = (z, x)
    cross, cross_to = (x, z), (x_to, z_to)

    def on_ring(g, r, cc):
        return dev(x, r, y, cc) if g == 0 else dev(r, z, y, cc)

    branched = []

    def remote(src, dst, send_sem, recv_sem, device):
        return pltpu.make_async_remote_copy(
            src_ref=src, dst_ref=dst, send_sem=send_sem, recv_sem=recv_sem,
            device_id=device, device_id_type=MESH,
        )

    def send(src, dst, send_sem, recv_sem, device):
        remote(src, dst, send_sem, recv_sem, device).start()

    def arrived(dst, sem):
        pltpu.make_async_copy(dst, dst, sem).wait()

    def left(src, sem):
        arrived(src, sem)

    def send_or_copy(src, dst, send_sem, recv_sem, device, own):
        copy = remote(src, dst, send_sem, recv_sem, device)

        @pl.when(own)
        def _():
            pltpu.make_async_copy(src, dst, recv_sem).start()

        @pl.when(jnp.logical_not(own))
        def _():
            copy.start()

        branched.append((copy, own))

    def drain():
        while branched:
            copy, own = branched.pop(0)

            @pl.when(jnp.logical_not(own))
            def _(copy=copy):
                copy.wait_send()

    def code_block(i):
        dy = (2, 1, 3, 0)[i // 2]
        cc = 1 - c if i % 2 == 0 else c
        return 2 * wrap(y + dy) + cc

    def code_copy(i):
        cols = pl.ds(pl.multiple_of(code_block(i) * COL, COL), COL)
        return pltpu.make_async_copy(codes.at[:, cols], codes_v.at[i % SLOTS], c_sem.at[i % SLOTS])

    act_copy = pltpu.make_async_copy(act, act_v, l_sem.at[0])
    act_copy.start()
    for i in range(SLOTS):
        code_copy(i).start()
    res_copy = pltpu.make_async_copy(residual, res_v, l_sem.at[1])
    res_copy.start()
    go_copy = pltpu.make_async_copy(grad_out, go_v, l_sem.at[2])
    go_copy.start()
    col_copy = pltpu.make_async_copy(
        col_code.at[:, pl.ds(pl.multiple_of(t * COL, COL), COL)], col_v, l_sem.at[3]
    )
    col_copy.start()

    barrier = pltpu.get_barrier_semaphore()
    greeted = 0

    def greet(device):
        pl.semaphore_signal(barrier, inc=1, device_id=device, device_id_type=MESH)

    for r in range(1, 8):
        greet({"tensor": lax.rem(t + r, 8), "seq": s})
        greeted += 1
    for g in range(2):
        for r in range(1, 4):
            for cc in range(2):
                greet(on_ring(g, wrap(ring[g] + r), cc))
                greeted += 1

    def place(g, a, ys):
        n = 4 * a + ys
        if g == 0:
            return n
        xo = lax.div(n, 3)
        return 4 * lax.rem(n, 3) + wrap(x - xo)

    def slab(g, a, ys, q, first, count):
        rows = pl.ds(pl.multiple_of((4 * q + first) * QT, QT), count * QT)
        cols = pl.ds(pl.multiple_of(place(g, a, ys) * UNIT, UNIT), UNIT)
        return taps.at[g, rows, cols]

    def tap_out(a, q, src):
        n = 4 * a + y
        for g in range(2):
            for e in range(2):
                j = 2 * c + e
                if g == 0:
                    to, pos = j, n
                else:
                    to, pos = lax.rem(j + lax.div(n, 3), 4), 4 * lax.rem(n, 3) + j
                rows = pl.ds(pl.multiple_of((4 * q + ring[g]) * QT, QT), QT)
                cols = pl.ds(pl.multiple_of(pos * UNIT, UNIT), UNIT)
                send_or_copy(
                    src.at[pl.ds(q * QT, QT), pl.ds((2 * e + g) * UNIT, UNIT)],
                    taps.at[g, rows, cols],
                    t_zs.at[g, a, q, e],
                    t_in.at[g, a, q],
                    on_ring(g, to, lax.div(ring[g], 2)),
                    jnp.logical_and(to == ring[g], lax.div(ring[g], 2) == c),
                )

    def tap_share(g, a, q, dy):
        here = slab(g, a, wrap(y + dy), q, 2 * c, 2)
        send(here, here, t_ps, t_pp.at[g, q], partner)

    def tap_own(a, q):
        for g in range(2):
            here = slab(g, a, y, q, 2 * c, 2)
            arrived(here, t_in.at[g, a, q])
            for way in range(2):
                send(here, here, t_ys.at[way], t_side.at[g, a, q, way], y_to[way])
            tap_share(g, a, q, 0)

    def tap_sides(a, q):
        for g in range(2):
            for way in range(2):
                dy = (3, 1)[way]
                ys = wrap(y + dy)
                arrived(slab(g, a, ys, q, 2 * c, 2), t_side.at[g, a, q, way])
                part = slab(g, a, ys, q, 2 * c + way, 1)
                send(part, part, t_fs.at[way], t_far.at[g, a, q], y_to[way])
                tap_share(g, a, q, dy)

    def tap_far(a, q):
        for g in range(2):
            arrived(slab(g, a, wrap(y + 2), q, 2 * c, 2), t_far.at[g, a, q])
            tap_share(g, a, q, 2)

    def tap_partner(q):
        for g in range(2):
            rows = pl.ds(pl.multiple_of((4 * q + 2 * (1 - c)) * QT, QT), 2 * QT)
            arrived(taps.at[g, rows], t_pp.at[g, q])

    def tap_left():
        left(taps.at[0], t_ps)
        for way in range(2):
            left(taps.at[0, pl.ds(0, 512)], t_ys.at[way])
            left(taps.at[0, pl.ds(0, 256)], t_fs.at[way])

    def w_block(g, p, half=None):
        if half is None:
            return wts.at[g, pl.ds(pl.multiple_of(p * XB, XB), XB)]
        n = XB // 2
        return wts.at[g, pl.ds(pl.multiple_of(p * XB + half * n, n), n)]

    def w_out():
        for e in range(3):
            for g in range(2):
                q = 3 * z + e
                if g == 0:
                    to, i = lax.rem(q, 4), lax.div(q, 4)
                else:
                    to, i = lax.rem(q + x, 4), e
                rows = pl.ds(pl.multiple_of((3 * cross[g] + i) * UNIT, UNIT), UNIT)
                send_or_copy(
                    weight.at[pl.ds((2 * e + g) * UNIT, UNIT)], wts.at[g, rows],
                    w_as.at[g, e], w_own.at[g], on_ring(g, to, c), to == ring[g],
                )

    def w_sides():
        for g in range(2):
            here = w_block(g, cross[g])
            arrived(here, w_own.at[g])
            for way in range(2):
                send(here, here, w_ss.at[g, way], w_side.at[g, way], cross_to[g][way])

    def w_forward():
        for g in range(2):
            for way in range(2):
                p = wrap(cross[g] + (3, 1)[way])
                arrived(w_block(g, p), w_side.at[g, way])
                half = w_block(g, p, way)
                send(half, half, w_fs.at[g, way], w_d2.at[g], cross_to[g][way])

    def w_far():
        for g in range(2):
            arrived(w_block(g, wrap(cross[g] + 2)), w_d2.at[g])

    def w_left():
        for g in range(2):
            for way in range(2):
                left(w_block(g, 0), w_ss.at[g, way])
                left(w_block(g, 0, 0), w_fs.at[g, way])

    def down_dot(i):
        code_copy(i).wait()
        part = dot(act_v[...], codes_v[i % SLOTS])
        n = i // 2
        if i % 2 == 0:
            d_ps[n] = part.astype(BF)
        else:
            d_own[n] = part
        if i + SLOTS < 8:
            code_copy(i + SLOTS).start()

    def down_share(n):
        send(d_ps.at[n], d_pr.at[n], dp_send.at[n], dp_recv.at[n], partner)

    def down_block(i):
        down_dot(i)
        if i % 2 == 0:
            down_share(i // 2)

    def down_far(h):
        for way in range(2):
            rows = slice(h * HT + way * FT, h * HT + way * FT + FT)
            d_hs[h, way] = (d_own[0, rows] + d_pr[0, rows].astype(F32)).astype(BF)
            send(d_hs.at[h, way], d_hr.at[h, way], dh_send.at[h, way], dh_recv.at[h, way], y_to[way])

    def down_sides(h):
        for way in range(2):
            n = 1 + way
            arrived(d_hr.at[h, way], dh_recv.at[h, way])
            for half in range(2):
                rows = slice(h * HT + half * FT, h * HT + half * FT + FT)
                value = d_own[n, rows] + d_pr[n, rows].astype(F32)
                if half == way:
                    value = value + d_hr[h, way].astype(F32)
                d_bs[h, way, half * FT : half * FT + FT] = value.astype(BF)
            send(d_bs.at[h, way], d_br.at[h, way], db_send.at[h, way], db_recv.at[h, way], y_to[way])

    def down_end(h):
        for way in range(2):
            arrived(d_br.at[h, way], db_recv.at[h, way])
        rows = slice(h * HT, h * HT + HT)
        row_full = jnp.broadcast_to(act_scale[:, rows], (128, HT)).T[:, :1]
        col_full = col_v[...].astype(F32) * QUANT_UNIT
        down = d_own[3, rows] + d_pr[3, rows].astype(F32)
        down = down + d_br[h, 0].astype(F32) + d_br[h, 1].astype(F32)
        high_v[rows] = (res_v[rows].astype(F32) + down * row_full * col_full).astype(BF)
        for q in range(h * NQ // 2, (h + 1) * NQ // 2):
            tap_out(2, q, high_v)

    def down_left():
        for n in range(4):
            left(d_ps.at[n], dp_send.at[n])
        for h in range(2):
            for way in range(2):
                left(d_hs.at[h, way], dh_send.at[h, way])
                left(d_bs.at[h, way], db_send.at[h, way])

    def join_start(q):
        tap_partner(q)
        for g in range(2):
            rows = pl.ds(4 * q * QT, 4 * QT)
            j_s[q, g] = dot(taps[g, rows], wts[g]).astype(BF)
            for r in (2, 1, 3):
                to = wrap(ring[g] + r)
                send(
                    j_s.at[q, g, pl.ds(pl.multiple_of(to * QT, QT), QT)], j_r.at[q, g, r - 1],
                    j_send, j_recv.at[q], on_ring(g, to, c),
                )

    def join_end(q):
        arrived(j_r.at[q], j_recv.at[q])
        rows = slice(q * QT, q * QT + QT)
        joined = jnp.zeros((QT, COL), F32)
        for g in range(2):
            joined = joined + j_s[q, g, pl.ds(pl.multiple_of(ring[g] * QT, QT), QT)].astype(F32)
            for r in range(3):
                joined = joined + j_r[q, g, r].astype(F32)
        j_v[rows] = joined
        grad_norm = go_v[rows].astype(F32) * gain[...]
        lane = lax.broadcasted_iota(jnp.int32, (QT, 128), 1)
        squares = jnp.sum(joined * joined, axis=1, keepdims=True)
        inner = jnp.sum(grad_norm * joined, axis=1, keepdims=True)
        both = jnp.where(lane == 0, squares, jnp.where(lane == 1, inner, 0.0))
        st_s[q] = both.T[:8]
        for r in range(1, 8):
            send(
                st_s.at[q], st_r.at[q, r - 1], st_send, st_recv.at[q],
                {"tensor": lax.rem(t + r, 8), "seq": s},
            )

    def g_piece(g, q, n, r):
        cols = pl.ds(pl.multiple_of((4 * q + r) * QT, QT), QT)
        return gt_v.at[g, pl.ds(n * CW, CW), cols]

    def norm(q):
        arrived(st_r.at[q], st_recv.at[q])
        rows = slice(q * QT, q * QT + QT)
        total = st_s[q]
        for r in range(7):
            total = total + st_r[q, r]
        both = jnp.concatenate([total, jnp.zeros((120, QT), F32)], axis=0).T
        inverse_rms = lax.rsqrt(both[:, 0:1] / D + 1e-05)
        projection = inverse_rms * both[:, 1:2] / D
        normed = j_v[rows] * inverse_rms
        grad_norm = go_v[rows].astype(F32) * gain[...]
        grad_joined = inverse_rms * (grad_norm - normed * projection)
        turned = grad_joined.T.astype(BF)
        for g in range(2):
            gt_v[g, :, pl.ds(pl.multiple_of((4 * q + ring[g]) * QT, QT), QT)] = turned
        for n in range(CHUNKS):
            for g in range(2):
                here = g_piece(g, q, n, ring[g])
                for r in (2, 1, 3):
                    send(
                        here, here, a_send, a_recv.at[g, q, n, r - 1],
                        on_ring(g, wrap(ring[g] + r), c),
                    )
        drafted_v[rows] = (normed * gain[...]).astype(BF)

    def grad_part(g, n, p):
        cols = pl.ds(pl.multiple_of(wrap(cross[g] + p) * XB, XB), XB)
        return dot(gt_v[g, n * CW : n * CW + CW], taps[g, :, cols])

    def grad_start(n):
        for g in range(2):
            for q in range(NQ):
                for r in range(1, 4):
                    arrived(g_piece(g, q, n, wrap(ring[g] - r)), a_recv.at[g, q, n, r - 1])
            part = grad_part(g, n, 2).astype(BF)
            for way in range(2):
                g_hs[n, g, way] = part[way * CH : way * CH + CH]
                send(
                    g_hs.at[n, g, way], g_hr.at[n, g, way], gh_send,
                    gh_recv.at[n, g, way], cross_to[g][way],
                )

    def grad_sides(n):
        for g in range(2):
            for way in range(2):
                part = grad_part(g, n, (1, 3)[way])
                arrived(g_hr.at[n, g, way], gh_recv.at[n, g, way])
                for half in range(2):
                    rows = slice(half * CH, half * CH + CH)
                    value = part[rows]
                    if half == way:
                        value = value + g_hr[n, g, way].astype(F32)
                    g_bs[n, g, way, rows] = value.astype(BF)
                send(
                    g_bs.at[n, g, way], g_br.at[n, g, way], gb_send,
                    gb_recv.at[n, g], cross_to[g][way],
                )

    def grad_own(n):
        for g in range(2):
            g_own[n, g] = grad_part(g, n, 0)

    def grad_end(n):
        for g in range(2):
            arrived(g_br.at[n, g], gb_recv.at[n, g])
            total = g_own[n, g] + g_br[n, g, 0].astype(F32) + g_br[n, g, 1].astype(F32)
            f_s[n, g] = total.T.astype(BF)
            for i in range(3):
                if g == 0:
                    q = 4 * i + z
                    to, e = lax.div(q, 3), lax.rem(q, 3)
                else:
                    to, e = wrap(x + z - i), i
                rows = pl.ds(pl.multiple_of((2 * e + g) * UNIT, UNIT), UNIT)
                send_or_copy(
                    f_s.at[n, g, pl.ds(i * UNIT, UNIT)],
                    grad_join.at[rows, pl.ds(n * CW, CW)],
                    f_send.at[n, g, i], f_recv.at[n], on_ring(g, to, c), to == ring[g],
                )

    act_copy.wait()
    down_dot(0)
    pl.semaphore_wait(barrier, greeted)
    tap_out(0, 0, tap_low)
    tap_out(1, 0, tap_mid)
    down_share(0)
    w_out()
    for q in range(1, NQ):
        tap_out(0, q, tap_low)
        tap_out(1, q, tap_mid)
    down_block(1)
    down_block(2)
    tap_own(0, 0)
    arrived(d_pr.at[0], dp_recv.at[0])
    down_far(0)
    down_far(1)
    down_block(3)
    tap_own(1, 0)
    w_sides()
    down_block(4)
    down_block(5)
    tap_own(0, 1)
    for n in (1, 2):
        arrived(d_pr.at[n], dp_recv.at[n])
    down_sides(0)
    down_sides(1)
    tap_sides(0, 0)
    down_block(6)
    tap_sides(1, 0)
    down_block(7)
    tap_own(1, 1)
    w_forward()
    tap_far(0, 0)
    tap_far(1, 0)
    arrived(d_pr.at[3], dp_recv.at[3])
    res_copy.wait()
    col_copy.wait()
    down_end(0)
    tap_sides(0, 1)
    down_end(1)
    tap_own(2, 0)
    tap_sides(1, 1)
    tap_own(2, 1)
    go_copy.wait()
    w_far()
    tap_sides(2, 0)
    tap_own(0, 2)
    tap_far(0, 1)
    tap_far(1, 1)
    tap_sides(2, 1)
    tap_own(1, 2)
    tap_far(2, 0)
    join_start(0)
    tap_own(2, 2)
    tap_far(2, 1)
    join_start(1)
    tap_sides(0, 2)
    tap_own(0, 3)
    tap_sides(1, 2)
    join_end(0)
    tap_own(1, 3)
    tap_sides(2, 2)
    tap_own(2, 3)
    norm(0)
    tap_far(0, 2)
    tap_far(1, 2)
    join_end(1)
    tap_sides(0, 3)
    tap_far(2, 2)
    join_start(2)
    norm(1)
    tap_sides(1, 3)
    tap_sides(2, 3)
    join_end(2)
    tap_far(0, 3)
    tap_far(1, 3)
    norm(2)
    tap_far(2, 3)
    join_start(3)
    drain()
    down_left()
    w_left()
    join_end(3)
    tap_left()
    norm(3)
    drafted_copy = pltpu.make_async_copy(drafted_v, drafted, l_sem.at[4])
    drafted_copy.start()
    for n in range(CHUNKS):
        grad_start(n)
    for n in range(CHUNKS):
        grad_sides(n)
        grad_own(n)
    left(j_r, j_send)
    left(st_r, st_send)
    left(taps.at[0, pl.ds(0, 1024)], a_send)
    for n in range(CHUNKS):
        grad_end(n)

    left(g_hs, gh_send)
    left(g_bs, gb_send)
    drain()
    drafted_copy.wait()
    for n in range(CHUNKS):
        arrived(grad_join.at[:, pl.ds(n * CW, CW)], f_recv.at[n])


def on_device(
    tap_low, tap_mid, residual_in, ffn_act, act_scale, down_codes, down_scale,
    join_weight, join_gain, grad_out,
):
    any_ = pl.BlockSpec(memory_space=pl.ANY)
    vmem = pl.BlockSpec(memory_space=pltpu.VMEM)
    V = pltpu.VMEM
    dma = lambda *shape: pltpu.SemaphoreType.DMA(shape)
    one = pltpu.SemaphoreType.DMA
    scratch = [
        V((TOK, HID), BF), V((SLOTS, HID, COL), BF), V((1, COL), jnp.int32),
        V((TOK, COL), BF), V((TOK, COL), BF),
        V((2, 4 * TOK, KG), BF), V((2, KG, COL), BF),
        V((4, TOK, COL), F32), V((4, TOK, COL), BF), V((4, TOK, COL), BF),
        V((2, 2, FT, COL), BF), V((2, 2, FT, COL), BF),
        V((2, 2, HT, COL), BF), V((2, 2, HT, COL), BF),
        V((TOK, COL), BF),
        V((NQ, 2, 4 * QT, COL), BF), V((NQ, 2, 3, QT, COL), BF),
        V((TOK, COL), F32), V((NQ, 8, QT), F32), V((NQ, 7, 8, QT), F32), V((TOK, COL), BF),
        V((2, COL, 4 * TOK), BF), V((CHUNKS, 2, CW, XB), F32),
        V((CHUNKS, 2, 2, CH, XB), BF), V((CHUNKS, 2, 2, CH, XB), BF),
        V((CHUNKS, 2, 2, CW, XB), BF), V((CHUNKS, 2, 2, CW, XB), BF),
        V((CHUNKS, 2, XB, CW), BF),
        dma(5), dma(SLOTS),
        dma(2, 3, NQ), dma(2, 3, NQ, 2), dma(2, 3, NQ), dma(2, NQ),
        dma(2, 3, NQ, 2), dma(2), dma(2), one,
        dma(2), dma(2, 3), dma(2, 2), dma(2), dma(2, 2), dma(2, 2),
        dma(4), dma(4), dma(2, 2), dma(2, 2), dma(2, 2), dma(2, 2),
        dma(NQ), one, dma(NQ), one, dma(2, NQ, CHUNKS, 3), one,
        dma(CHUNKS, 2, 2), one, dma(CHUNKS, 2), one,
        dma(CHUNKS), dma(CHUNKS, 2, 3),
    ]
    return pl.pallas_call(
        body,
        out_shape=(
            jax.ShapeDtypeStruct((TOK, COL), BF),
            jax.ShapeDtypeStruct((2 * XB, COL), BF),
        ),
        in_specs=[any_, any_, any_, any_, vmem, any_, any_, any_, vmem, any_],
        out_specs=(any_, any_),
        scratch_shapes=scratch,
        compiler_params=pltpu.CompilerParams(
            collective_id=0, has_side_effects=True, vmem_limit_bytes=63 * 1024 * 1024
        ),
        cost_estimate=pl.CostEstimate(
            flops=20_400_000_000, bytes_accessed=30_000_000, transcendentals=0
        ),
        name="tapped_join",
    )(
        tap_low, tap_mid, residual_in, ffn_act, act_scale.reshape(1, TOK), down_codes,
        down_scale.reshape(1, D), join_weight, join_gain.reshape(1, COL), grad_out,
    )


def solution(mesh):
    return jax.shard_map(
        on_device,
        mesh=mesh,
        in_specs=(
            P("seq", "tensor"),
            P("seq", "tensor"),
            P("seq", "tensor"),
            P("seq", "tensor"),
            P("seq"),
            P("tensor", None),
            P(),
            P("seq", "tensor"),
            P("tensor"),
            P("seq", "tensor"),
        ),
        out_specs=(P("seq", "tensor"), P("seq", "tensor")),
        check_vma=False,
    )
```

```python
import jax
import jax.numpy as jnp
from jax import lax
from jax.experimental import pallas as pl
from jax.experimental.pallas import tpu as pltpu
from jax.sharding import PartitionSpec as P

D = 4096
QUANT_UNIT = 2.0 ** (-19)
BF = jnp.bfloat16
F32 = jnp.float32
TOK = 512
NQ = 4
QT = TOK // NQ
HT = TOK // 2
FT = HT // 2
COL = 512
UNIT = 128
HID = 1792
SLOTS = 4
CHUNKS = 2
CW = COL // CHUNKS
CH = CW // 2
XB = 3 * UNIT
KG = 12 * UNIT
MESH = pl.DeviceIdType.MESH


def dot(a, b):
    return jnp.dot(a, b, preferred_element_type=F32)


def body(
    tap_low, tap_mid, residual, act, act_scale, codes, col_code, weight, gain, grad_out,
    drafted, grad_join,
    act_v, codes_v, col_v, res_v, go_v, taps, wts,
    d_own, d_ps, d_pr, d_hs, d_hr, d_bs, d_br, high_v,
    j_s, j_r, j_v, st_s, st_r, drafted_v,
    gt_v, g_own, g_hs, g_hr, g_bs, g_br, f_s,
    l_sem, c_sem,
    t_in, t_side, t_far, t_pp, t_zs, t_ys, t_fs, t_ps,
    w_own, w_as, w_side, w_d2, w_ss, w_fs,
    dp_recv, dp_send, dh_recv, dh_send, db_recv, db_send,
    j_recv, j_send, st_recv, st_send, a_recv, a_send,
    gh_recv, gh_send, gb_recv, gb_send,
    f_recv, f_send,
):
    s = lax.axis_index("seq")
    t = lax.axis_index("tensor")
    x, z = lax.div(s, 4), lax.rem(s, 4)
    y, c = lax.div(t, 2), lax.rem(t, 2)

    def wrap(v):
        return lax.rem(v + 4, 4)

    def dev(xx, zz, yy, cc):
        return {"tensor": 2 * yy + cc, "seq": 4 * xx + zz}

    partner = dev(x, z, y, 1 - c)
    y_to = (dev(x, z, wrap(y + 1), c), dev(x, z, wrap(y - 1), c))
    z_to = (dev(x, wrap(z + 1), y, c), dev(x, wrap(z - 1), y, c))
    x_to = (dev(wrap(x + 1), z, y, c), dev(wrap(x - 1), z, y, c))
    ring = (z, x)
    cross, cross_to = (x, z), (x_to, z_to)

    def on_ring(g, r, cc):
        return dev(x, r, y, cc) if g == 0 else dev(r, z, y, cc)

    branched = []

    def remote(src, dst, send_sem, recv_sem, device):
        return pltpu.make_async_remote_copy(
            src_ref=src, dst_ref=dst, send_sem=send_sem, recv_sem=recv_sem,
            device_id=device, device_id_type=MESH,
        )

    def send(src, dst, send_sem, recv_sem, device):
        remote(src, dst, send_sem, recv_sem, device).start()

    def arrived(dst, sem):
        pltpu.make_async_copy(dst, dst, sem).wait()

    def left(src, sem):
        arrived(src, sem)

    def send_or_copy(src, dst, send_sem, recv_sem, device, own):
        copy = remote(src, dst, send_sem, recv_sem, device)

        @pl.when(own)
        def _():
            pltpu.make_async_copy(src, dst, recv_sem).start()

        @pl.when(jnp.logical_not(own))
        def _():
            copy.start()

        branched.append((copy, own))

    def drain():
        while branched:
            copy, own = branched.pop(0)

            @pl.when(jnp.logical_not(own))
            def _(copy=copy):
                copy.wait_send()

    def code_block(i):
        dy = (2, 1, 3, 0)[i // 2]
        cc = 1 - c if i % 2 == 0 else c
        return 2 * wrap(y + dy) + cc

    def code_copy(i):
        cols = pl.ds(pl.multiple_of(code_block(i) * COL, COL), COL)
        return pltpu.make_async_copy(codes.at[:, cols], codes_v.at[i % SLOTS], c_sem.at[i % SLOTS])

    act_copy = pltpu.make_async_copy(act, act_v, l_sem.at[0])
    act_copy.start()
    for i in range(SLOTS):
        code_copy(i).start()
    res_copy = pltpu.make_async_copy(residual, res_v, l_sem.at[1])
    res_copy.start()
    go_copy = pltpu.make_async_copy(grad_out, go_v, l_sem.at[2])
    go_copy.start()
    col_copy = pltpu.make_async_copy(
        col_code.at[:, pl.ds(pl.multiple_of(t * COL, COL), COL)], col_v, l_sem.at[3]
    )
    col_copy.start()

    barrier = pltpu.get_barrier_semaphore()
    greeted = 0

    def greet(device):
        pl.semaphore_signal(barrier, inc=1, device_id=device, device_id_type=MESH)

    for r in range(1, 8):
        greet({"tensor": lax.rem(t + r, 8), "seq": s})
        greeted += 1
    for g in range(2):
        for r in range(1, 4):
            for cc in range(2):
                greet(on_ring(g, wrap(ring[g] + r), cc))
                greeted += 1

    def place(g, a, ys):
        n = 4 * a + ys
        if g == 0:
            return n
        xo = lax.div(n, 3)
        return 4 * lax.rem(n, 3) + wrap(x - xo)

    def slab(g, a, ys, q, first, count):
        rows = pl.ds(pl.multiple_of((4 * q + first) * QT, QT), count * QT)
        cols = pl.ds(pl.multiple_of(place(g, a, ys) * UNIT, UNIT), UNIT)
        return taps.at[g, rows, cols]

    def tap_out(a, q, src):
        n = 4 * a + y
        for g in range(2):
            for e in range(2):
                j = 2 * c + e
                if g == 0:
                    to, pos = j, n
                else:
                    to, pos = lax.rem(j + lax.div(n, 3), 4), 4 * lax.rem(n, 3) + j
                rows = pl.ds(pl.multiple_of((4 * q + ring[g]) * QT, QT), QT)
                cols = pl.ds(pl.multiple_of(pos * UNIT, UNIT), UNIT)
                send_or_copy(
                    src.at[pl.ds(q * QT, QT), pl.ds((2 * e + g) * UNIT, UNIT)],
                    taps.at[g, rows, cols],
                    t_zs.at[g, a, q, e],
                    t_in.at[g, a, q],
                    on_ring(g, to, lax.div(ring[g], 2)),
                    jnp.logical_and(to == ring[g], lax.div(ring[g], 2) == c),
                )

    def tap_share(g, a, q, dy):
        here = slab(g, a, wrap(y + dy), q, 2 * c, 2)
        send(here, here, t_ps, t_pp.at[g, q], partner)

    def tap_own(a, q):
        for g in range(2):
            here = slab(g, a, y, q, 2 * c, 2)
            arrived(here, t_in.at[g, a, q])
            for way in range(2):
                send(here, here, t_ys.at[way], t_side.at[g, a, q, way], y_to[way])
            tap_share(g, a, q, 0)

    def tap_sides(a, q):
        for g in range(2):
            for way in range(2):
                dy = (3, 1)[way]
                ys = wrap(y + dy)
                arrived(slab(g, a, ys, q, 2 * c, 2), t_side.at[g, a, q, way])
                part = slab(g, a, ys, q, 2 * c + way, 1)
                send(part, part, t_fs.at[way], t_far.at[g, a, q], y_to[way])
                tap_share(g, a, q, dy)

    def tap_far(a, q):
        for g in range(2):
            arrived(slab(g, a, wrap(y + 2), q, 2 * c, 2), t_far.at[g, a, q])
            tap_share(g, a, q, 2)

    def tap_partner(q):
        for g in range(2):
            rows = pl.ds(pl.multiple_of((4 * q + 2 * (1 - c)) * QT, QT), 2 * QT)
            arrived(taps.at[g, rows], t_pp.at[g, q])

    def tap_left():
        left(taps.at[0], t_ps)
        for way in range(2):
            left(taps.at[0, pl.ds(0, 512)], t_ys.at[way])
            left(taps.at[0, pl.ds(0, 256)], t_fs.at[way])

    def w_block(g, p, half=None):
        if half is None:
            return wts.at[g, pl.ds(pl.multiple_of(p * XB, XB), XB)]
        n = XB // 2
        return wts.at[g, pl.ds(pl.multiple_of(p * XB + half * n, n), n)]

    def w_out():
        for e in range(3):
            for g in range(2):
                q = 3 * z + e
                if g == 0:
                    to, i = lax.rem(q, 4), lax.div(q, 4)
                else:
                    to, i = lax.rem(q + x, 4), e
                rows = pl.ds(pl.multiple_of((3 * cross[g] + i) * UNIT, UNIT), UNIT)
                send_or_copy(
                    weight.at[pl.ds((2 * e + g) * UNIT, UNIT)], wts.at[g, rows],
                    w_as.at[g, e], w_own.at[g], on_ring(g, to, c), to == ring[g],
                )

    def w_sides():
        for g in range(2):
            here = w_block(g, cross[g])
            arrived(here, w_own.at[g])
            for way in range(2):
                send(here, here, w_ss.at[g, way], w_side.at[g, way], cross_to[g][way])

    def w_forward():
        for g in range(2):
            for way in range(2):
                p = wrap(cross[g] + (3, 1)[way])
                arrived(w_block(g, p), w_side.at[g, way])
                half = w_block(g, p, way)
                send(half, half, w_fs.at[g, way], w_d2.at[g], cross_to[g][way])

    def w_far():
        for g in range(2):
            arrived(w_block(g, wrap(cross[g] + 2)), w_d2.at[g])

    def w_left():
        for g in range(2):
            for way in range(2):
                left(w_block(g, 0), w_ss.at[g, way])
                left(w_block(g, 0, 0), w_fs.at[g, way])

    def down_dot(i):
        code_copy(i).wait()
        part = dot(act_v[...], codes_v[i % SLOTS])
        n = i // 2
        if i % 2 == 0:
            d_ps[n] = part.astype(BF)
        else:
            d_own[n] = part
        if i + SLOTS < 8:
            code_copy(i + SLOTS).start()

    def down_share(n):
        send(d_ps.at[n], d_pr.at[n], dp_send.at[n], dp_recv.at[n], partner)

    def down_block(i):
        down_dot(i)
        if i % 2 == 0:
            down_share(i // 2)

    def down_far(h):
        for way in range(2):
            rows = slice(h * HT + way * FT, h * HT + way * FT + FT)
            d_hs[h, way] = (d_own[0, rows] + d_pr[0, rows].astype(F32)).astype(BF)
            send(d_hs.at[h, way], d_hr.at[h, way], dh_send.at[h, way], dh_recv.at[h, way], y_to[way])

    def down_sides(h):
        for way in range(2):
            n = 1 + way
            arrived(d_hr.at[h, way], dh_recv.at[h, way])
            for half in range(2):
                rows = slice(h * HT + half * FT, h * HT + half * FT + FT)
                value = d_own[n, rows] + d_pr[n, rows].astype(F32)
                if half == way:
                    value = value + d_hr[h, way].astype(F32)
                d_bs[h, way, half * FT : half * FT + FT] = value.astype(BF)
            send(d_bs.at[h, way], d_br.at[h, way], db_send.at[h, way], db_recv.at[h, way], y_to[way])

    def down_end(h):
        for way in range(2):
            arrived(d_br.at[h, way], db_recv.at[h, way])
        rows = slice(h * HT, h * HT + HT)
        row_full = jnp.broadcast_to(act_scale[:, rows], (128, HT)).T[:, :1]
        col_full = col_v[...].astype(F32) * QUANT_UNIT
        down = d_own[3, rows] + d_pr[3, rows].astype(F32)
        down = down + d_br[h, 0].astype(F32) + d_br[h, 1].astype(F32)
        high_v[rows] = (res_v[rows].astype(F32) + down * row_full * col_full).astype(BF)
        for q in range(h * NQ // 2, (h + 1) * NQ // 2):
            tap_out(2, q, high_v)

    def down_left():
        for n in range(4):
            left(d_ps.at[n], dp_send.at[n])
        for h in range(2):
            for way in range(2):
                left(d_hs.at[h, way], dh_send.at[h, way])
                left(d_bs.at[h, way], db_send.at[h, way])

    def join_start(q):
        tap_partner(q)
        for g in range(2):
            rows = pl.ds(4 * q * QT, 4 * QT)
            j_s[q, g] = dot(taps[g, rows], wts[g]).astype(BF)
            for r in (2, 1, 3):
                to = wrap(ring[g] + r)
                send(
                    j_s.at[q, g, pl.ds(pl.multiple_of(to * QT, QT), QT)], j_r.at[q, g, r - 1],
                    j_send, j_recv.at[q], on_ring(g, to, c),
                )

    def join_end(q):
        arrived(j_r.at[q], j_recv.at[q])
        rows = slice(q * QT, q * QT + QT)
        joined = jnp.zeros((QT, COL), F32)
        for g in range(2):
            joined = joined + j_s[q, g, pl.ds(pl.multiple_of(ring[g] * QT, QT), QT)].astype(F32)
            for r in range(3):
                joined = joined + j_r[q, g, r].astype(F32)
        j_v[rows] = joined
        grad_norm = go_v[rows].astype(F32) * gain[...]
        lane = lax.broadcasted_iota(jnp.int32, (QT, 128), 1)
        squares = jnp.sum(joined * joined, axis=1, keepdims=True)
        inner = jnp.sum(grad_norm * joined, axis=1, keepdims=True)
        both = jnp.where(lane == 0, squares, jnp.where(lane == 1, inner, 0.0))
        st_s[q] = both.T[:8]
        for r in range(1, 8):
            send(
                st_s.at[q], st_r.at[q, r - 1], st_send, st_recv.at[q],
                {"tensor": lax.rem(t + r, 8), "seq": s},
            )

    def g_piece(g, q, n, r):
        cols = pl.ds(pl.multiple_of((4 * q + r) * QT, QT), QT)
        return gt_v.at[g, pl.ds(n * CW, CW), cols]

    def norm(q):
        arrived(st_r.at[q], st_recv.at[q])
        rows = slice(q * QT, q * QT + QT)
        total = st_s[q]
        for r in range(7):
            total = total + st_r[q, r]
        both = jnp.concatenate([total, jnp.zeros((120, QT), F32)], axis=0).T
        inverse_rms = lax.rsqrt(both[:, 0:1] / D + 1e-05)
        projection = inverse_rms * both[:, 1:2] / D
        normed = j_v[rows] * inverse_rms
        grad_norm = go_v[rows].astype(F32) * gain[...]
        grad_joined = inverse_rms * (grad_norm - normed * projection)
        turned = grad_joined.T.astype(BF)
        for g in range(2):
            gt_v[g, :, pl.ds(pl.multiple_of((4 * q + ring[g]) * QT, QT), QT)] = turned
        for n in range(CHUNKS):
            for g in range(2):
                here = g_piece(g, q, n, ring[g])
                for r in (2, 1, 3):
                    send(
                        here, here, a_send, a_recv.at[g, q, n, r - 1],
                        on_ring(g, wrap(ring[g] + r), c),
                    )
        drafted_v[rows] = (normed * gain[...]).astype(BF)

    def grad_part(g, n, p):
        cols = pl.ds(pl.multiple_of(wrap(cross[g] + p) * XB, XB), XB)
        return dot(gt_v[g, n * CW : n * CW + CW], taps[g, :, cols])

    def grad_start(n):
        for g in range(2):
            for q in range(NQ):
                for r in range(1, 4):
                    arrived(g_piece(g, q, n, wrap(ring[g] - r)), a_recv.at[g, q, n, r - 1])
            part = grad_part(g, n, 2).astype(BF)
            for way in range(2):
                g_hs[n, g, way] = part[way * CH : way * CH + CH]
                send(
                    g_hs.at[n, g, way], g_hr.at[n, g, way], gh_send,
                    gh_recv.at[n, g, way], cross_to[g][way],
                )

    def grad_sides(n):
        for g in range(2):
            for way in range(2):
                part = grad_part(g, n, (1, 3)[way])
                arrived(g_hr.at[n, g, way], gh_recv.at[n, g, way])
                for half in range(2):
                    rows = slice(half * CH, half * CH + CH)
                    value = part[rows]
                    if half == way:
                        value = value + g_hr[n, g, way].astype(F32)
                    g_bs[n, g, way, rows] = value.astype(BF)
                send(
                    g_bs.at[n, g, way], g_br.at[n, g, way], gb_send,
                    gb_recv.at[n, g], cross_to[g][way],
                )

    def grad_own(n):
        for g in range(2):
            g_own[n, g] = grad_part(g, n, 0)

    def grad_end(n):
        for g in range(2):
            arrived(g_br.at[n, g], gb_recv.at[n, g])
            total = g_own[n, g] + g_br[n, g, 0].astype(F32) + g_br[n, g, 1].astype(F32)
            f_s[n, g] = total.T.astype(BF)
            for i in range(3):
                if g == 0:
                    q = 4 * i + z
                    to, e = lax.div(q, 3), lax.rem(q, 3)
                else:
                    to, e = wrap(x + z - i), i
                rows = pl.ds(pl.multiple_of((2 * e + g) * UNIT, UNIT), UNIT)
                send_or_copy(
                    f_s.at[n, g, pl.ds(i * UNIT, UNIT)],
                    grad_join.at[rows, pl.ds(n * CW, CW)],
                    f_send.at[n, g, i], f_recv.at[n], on_ring(g, to, c), to == ring[g],
                )

    act_copy.wait()
    down_dot(0)
    pl.semaphore_wait(barrier, greeted)
    tap_out(0, 0, tap_low)
    tap_out(1, 0, tap_mid)
    down_share(0)
    w_out()
    for q in range(1, NQ):
        tap_out(0, q, tap_low)
        tap_out(1, q, tap_mid)

    down_block(1)
    down_block(2)
    tap_own(0, 0)
    arrived(d_pr.at[0], dp_recv.at[0])
    down_far(0)
    down_far(1)
    down_block(3)
    tap_own(1, 0)
    w_sides()
    down_block(4)
    down_block(5)
    for n in (1, 2):
        arrived(d_pr.at[n], dp_recv.at[n])
    down_sides(0)
    down_sides(1)
    tap_own(0, 1)
    tap_sides(0, 0)
    down_block(6)
    tap_sides(1, 0)
    down_block(7)
    tap_own(1, 1)
    w_forward()
    tap_far(0, 0)
    tap_far(1, 0)
    arrived(d_pr.at[3], dp_recv.at[3])
    res_copy.wait()
    col_copy.wait()
    down_end(0)
    tap_sides(0, 1)
    down_end(1)
    tap_own(2, 0)
    tap_sides(1, 1)
    w_far()
    go_copy.wait()
    tap_sides(2, 0)
    tap_own(2, 1)
    tap_far(0, 1)
    tap_far(1, 1)
    tap_own(0, 2)
    tap_far(2, 0)
    join_start(0)
    tap_sides(2, 1)
    tap_own(1, 2)
    tap_own(2, 2)
    tap_far(2, 1)
    join_start(1)
    tap_sides(0, 2)
    join_end(0)
    tap_sides(1, 2)
    tap_own(0, 3)
    tap_sides(2, 2)
    norm(0)
    tap_own(1, 3)
    tap_far(0, 2)
    tap_own(2, 3)
    join_end(1)
    tap_far(1, 2)
    tap_far(2, 2)
    join_start(2)
    tap_sides(0, 3)
    norm(1)
    tap_sides(1, 3)
    tap_sides(2, 3)
    tap_far(0, 3)
    join_end(2)
    tap_far(1, 3)
    tap_far(2, 3)
    join_start(3)
    norm(2)
    drain()
    down_left()
    w_left()
    join_end(3)
    tap_left()
    norm(3)

    drafted_copy = pltpu.make_async_copy(drafted_v, drafted, l_sem.at[4])
    drafted_copy.start()
    for n in range(CHUNKS):
        grad_start(n)
    for n in range(CHUNKS):
        grad_sides(n)
        grad_own(n)
    left(j_r, j_send)
    left(st_r, st_send)
    left(taps.at[0, pl.ds(0, 1024)], a_send)
    for n in range(CHUNKS):
        grad_end(n)

    left(g_hs, gh_send)
    left(g_bs, gb_send)
    drain()
    drafted_copy.wait()
    for n in range(CHUNKS):
        arrived(grad_join.at[:, pl.ds(n * CW, CW)], f_recv.at[n])


def hand_on(drafted, grad_join, drafted_out, grad_join_out):
    drafted_out[...] = drafted[...]
    grad_join_out[...] = grad_join[...]


def on_device(
    tap_low, tap_mid, residual_in, ffn_act, act_scale, down_codes, down_scale,
    join_weight, join_gain, grad_out,
):
    any_ = pl.BlockSpec(memory_space=pl.ANY)
    vmem = pl.BlockSpec(memory_space=pltpu.VMEM)
    V = pltpu.VMEM
    dma = lambda *shape: pltpu.SemaphoreType.DMA(shape)
    one = pltpu.SemaphoreType.DMA
    scratch = [
        V((TOK, HID), BF), V((SLOTS, HID, COL), BF), V((1, COL), jnp.int32),
        V((TOK, COL), BF), V((TOK, COL), BF),
        V((2, 4 * TOK, KG), BF), V((2, KG, COL), BF),
        V((4, TOK, COL), F32), V((4, TOK, COL), BF), V((4, TOK, COL), BF),
        V((2, 2, FT, COL), BF), V((2, 2, FT, COL), BF),
        V((2, 2, HT, COL), BF), V((2, 2, HT, COL), BF),
        V((TOK, COL), BF),
        V((NQ, 2, 4 * QT, COL), BF), V((NQ, 2, 3, QT, COL), BF),
        V((TOK, COL), F32), V((NQ, 8, QT), F32), V((NQ, 7, 8, QT), F32), V((TOK, COL), BF),
        V((2, COL, 4 * TOK), BF), V((CHUNKS, 2, CW, XB), F32),
        V((CHUNKS, 2, 2, CH, XB), BF), V((CHUNKS, 2, 2, CH, XB), BF),
        V((CHUNKS, 2, 2, CW, XB), BF), V((CHUNKS, 2, 2, CW, XB), BF),
        V((CHUNKS, 2, XB, CW), BF),
        dma(5), dma(SLOTS),
        dma(2, 3, NQ), dma(2, 3, NQ, 2), dma(2, 3, NQ), dma(2, NQ),
        dma(2, 3, NQ, 2), dma(2), dma(2), one,
        dma(2), dma(2, 3), dma(2, 2), dma(2), dma(2, 2), dma(2, 2),
        dma(4), dma(4), dma(2, 2), dma(2, 2), dma(2, 2), dma(2, 2),
        dma(NQ), one, dma(NQ), one, dma(2, NQ, CHUNKS, 3), one,
        dma(CHUNKS, 2, 2), one, dma(CHUNKS, 2), one,
        dma(CHUNKS), dma(CHUNKS, 2, 3),
    ]
    shapes = (
        jax.ShapeDtypeStruct((TOK, COL), BF),
        jax.ShapeDtypeStruct((2 * XB, COL), BF),
    )
    results = pl.pallas_call(
        body,
        out_shape=shapes,
        in_specs=[any_, any_, any_, any_, vmem, any_, any_, any_, vmem, any_],
        out_specs=(any_, any_),
        scratch_shapes=scratch,
        compiler_params=pltpu.CompilerParams(
            collective_id=0, has_side_effects=True, vmem_limit_bytes=63 * 1024 * 1024
        ),
        cost_estimate=pl.CostEstimate(
            flops=20_400_000_000, bytes_accessed=30_000_000, transcendentals=0
        ),
        name="tapped_join",
    )(
        tap_low, tap_mid, residual_in, ffn_act, act_scale.reshape(1, TOK), down_codes,
        down_scale.reshape(1, D), join_weight, join_gain.reshape(1, COL), grad_out,
    )
    return pl.pallas_call(
        hand_on,
        out_shape=shapes,
        in_specs=[vmem, vmem],
        out_specs=(vmem, vmem),
        name="hand_on",
    )(*results)


def solution(mesh):
    return jax.shard_map(
        on_device,
        mesh=mesh,
        in_specs=(
            P("seq", "tensor"),
            P("seq", "tensor"),
            P("seq", "tensor"),
            P("seq", "tensor"),
            P("seq"),
            P("tensor", None),
            P(),
            P("seq", "tensor"),
            P("tensor"),
            P("seq", "tensor"),
        ),
        out_specs=(P("seq", "tensor"), P("seq", "tensor")),
        check_vma=False,
    )
```

```python
import jax
import jax.numpy as jnp
from jax import lax
from jax.experimental import pallas as pl
from jax.experimental.pallas import tpu as pltpu
from jax.sharding import PartitionSpec as P

D = 4096
QUANT_UNIT = 2.0 ** (-19)
BF = jnp.bfloat16
F32 = jnp.float32
TOK = 512
NQ = 4
QT = TOK // NQ
HT = TOK // 2
FT = HT // 2
COL = 512
UNIT = 128
HID = 1792
SLOTS = 4
CHUNKS = 2
CW = COL // CHUNKS
CH = CW // 2
XB = 3 * UNIT
KG = 12 * UNIT
MESH = pl.DeviceIdType.MESH


def dot(a, b):
    return jnp.dot(a, b, preferred_element_type=F32)


def body(
    tap_low, tap_mid, residual, act, act_scale, codes, col_code, weight, gain, grad_out,
    drafted, grad_join,
    act_v, codes_v, col_v, res_v, go_v, taps, wts,
    d_own, d_ps, d_pr, d_hs, d_hr, d_bs, d_br, high_v,
    j_s, j_r, j_v, st_s, st_r, drafted_v,
    gt_v, g_own, g_hs, g_hr, g_bs, g_br, f_s,
    l_sem, c_sem,
    t_in, t_side, t_far, t_pp, t_zs, t_ys, t_fs, t_ps,
    w_own, w_as, w_side, w_d2, w_ss, w_fs,
    dp_recv, dp_send, dh_recv, dh_send, db_recv, db_send,
    j_recv, j_send, st_recv, st_send, a_recv, a_send,
    gh_recv, gh_send, gb_recv, gb_send,
    f_recv, f_send,
):
    s = lax.axis_index("seq")
    t = lax.axis_index("tensor")
    x, z = lax.div(s, 4), lax.rem(s, 4)
    y, c = lax.div(t, 2), lax.rem(t, 2)

    def wrap(v):
        return lax.rem(v + 4, 4)

    def dev(xx, zz, yy, cc):
        return {"tensor": 2 * yy + cc, "seq": 4 * xx + zz}

    partner = dev(x, z, y, 1 - c)
    y_to = (dev(x, z, wrap(y + 1), c), dev(x, z, wrap(y - 1), c))
    z_to = (dev(x, wrap(z + 1), y, c), dev(x, wrap(z - 1), y, c))
    x_to = (dev(wrap(x + 1), z, y, c), dev(wrap(x - 1), z, y, c))
    ring = (z, x)
    cross, cross_to = (x, z), (x_to, z_to)

    def on_ring(g, r, cc):
        return dev(x, r, y, cc) if g == 0 else dev(r, z, y, cc)

    branched = []

    def remote(src, dst, send_sem, recv_sem, device):
        return pltpu.make_async_remote_copy(
            src_ref=src, dst_ref=dst, send_sem=send_sem, recv_sem=recv_sem,
            device_id=device, device_id_type=MESH,
        )

    def send(src, dst, send_sem, recv_sem, device):
        remote(src, dst, send_sem, recv_sem, device).start()

    def arrived(dst, sem):
        pltpu.make_async_copy(dst, dst, sem).wait()

    def left(src, sem):
        arrived(src, sem)

    def send_or_copy(src, dst, send_sem, recv_sem, device, own):
        copy = remote(src, dst, send_sem, recv_sem, device)

        @pl.when(own)
        def _():
            pltpu.make_async_copy(src, dst, recv_sem).start()

        @pl.when(jnp.logical_not(own))
        def _():
            copy.start()

        branched.append((copy, own))

    def drain():
        while branched:
            copy, own = branched.pop(0)

            @pl.when(jnp.logical_not(own))
            def _(copy=copy):
                copy.wait_send()

    def code_block(i):
        dy = (2, 1, 3, 0)[i // 2]
        cc = 1 - c if i % 2 == 0 else c
        return 2 * wrap(y + dy) + cc

    def code_copy(i):
        cols = pl.ds(pl.multiple_of(code_block(i) * COL, COL), COL)
        return pltpu.make_async_copy(codes.at[:, cols], codes_v.at[i % SLOTS], c_sem.at[i % SLOTS])

    barrier = pltpu.get_barrier_semaphore()
    greeted = 0

    def greet(device):
        pl.semaphore_signal(barrier, inc=1, device_id=device, device_id_type=MESH)

    for r in range(1, 8):
        greet({"tensor": lax.rem(t + r, 8), "seq": s})
        greeted += 1
    for g in range(2):
        for r in range(1, 4):
            for cc in range(2):
                greet(on_ring(g, wrap(ring[g] + r), cc))
                greeted += 1

    act_copy = pltpu.make_async_copy(act, act_v, l_sem.at[0])
    act_copy.start()
    for i in range(SLOTS):
        code_copy(i).start()
    res_copy = pltpu.make_async_copy(residual, res_v, l_sem.at[1])
    res_copy.start()
    go_copy = pltpu.make_async_copy(grad_out, go_v, l_sem.at[2])
    go_copy.start()
    col_copy = pltpu.make_async_copy(
        col_code.at[:, pl.ds(pl.multiple_of(t * COL, COL), COL)], col_v, l_sem.at[3]
    )
    col_copy.start()

    def place(g, a, ys):
        n = 4 * a + ys
        if g == 0:
            return n
        xo = lax.div(n, 3)
        return 4 * lax.rem(n, 3) + wrap(x - xo)

    def slab(g, a, ys, q, first, count):
        rows = pl.ds(pl.multiple_of((4 * q + first) * QT, QT), count * QT)
        cols = pl.ds(pl.multiple_of(place(g, a, ys) * UNIT, UNIT), UNIT)
        return taps.at[g, rows, cols]

    def tap_out(a, q, src):
        n = 4 * a + y
        for g in range(2):
            for e in range(2):
                j = 2 * c + e
                if g == 0:
                    to, pos = j, n
                else:
                    to, pos = lax.rem(j + lax.div(n, 3), 4), 4 * lax.rem(n, 3) + j
                rows = pl.ds(pl.multiple_of((4 * q + ring[g]) * QT, QT), QT)
                cols = pl.ds(pl.multiple_of(pos * UNIT, UNIT), UNIT)
                send_or_copy(
                    src.at[pl.ds(q * QT, QT), pl.ds((2 * e + g) * UNIT, UNIT)],
                    taps.at[g, rows, cols],
                    t_zs.at[g, a, q, e],
                    t_in.at[g, a, q],
                    on_ring(g, to, lax.div(ring[g], 2)),
                    jnp.logical_and(to == ring[g], lax.div(ring[g], 2) == c),
                )

    def tap_share(g, a, q, dy):
        here = slab(g, a, wrap(y + dy), q, 2 * c, 2)
        send(here, here, t_ps, t_pp.at[g, q], partner)

    def tap_own(a, q):
        for g in range(2):
            here = slab(g, a, y, q, 2 * c, 2)
            arrived(here, t_in.at[g, a, q])
            for way in range(2):
                send(here, here, t_ys.at[way], t_side.at[g, a, q, way], y_to[way])
            tap_share(g, a, q, 0)

    def tap_sides(a, q):
        for g in range(2):
            for way in range(2):
                dy = (3, 1)[way]
                ys = wrap(y + dy)
                arrived(slab(g, a, ys, q, 2 * c, 2), t_side.at[g, a, q, way])
                part = slab(g, a, ys, q, 2 * c + way, 1)
                send(part, part, t_fs.at[way], t_far.at[g, a, q], y_to[way])
                tap_share(g, a, q, dy)

    def tap_far(a, q):
        for g in range(2):
            arrived(slab(g, a, wrap(y + 2), q, 2 * c, 2), t_far.at[g, a, q])
            tap_share(g, a, q, 2)

    def tap_partner(q):
        for g in range(2):
            rows = pl.ds(pl.multiple_of((4 * q + 2 * (1 - c)) * QT, QT), 2 * QT)
            arrived(taps.at[g, rows], t_pp.at[g, q])

    def tap_left():
        left(taps.at[0], t_ps)
        for way in range(2):
            left(taps.at[0, pl.ds(0, 512)], t_ys.at[way])
            left(taps.at[0, pl.ds(0, 256)], t_fs.at[way])

    def w_block(g, p, half=None):
        if half is None:
            return wts.at[g, pl.ds(pl.multiple_of(p * XB, XB), XB)]
        n = XB // 2
        return wts.at[g, pl.ds(pl.multiple_of(p * XB + half * n, n), n)]

    def w_out():
        for e in range(3):
            for g in range(2):
                q = 3 * z + e
                if g == 0:
                    to, i = lax.rem(q, 4), lax.div(q, 4)
                else:
                    to, i = lax.rem(q + x, 4), e
                rows = pl.ds(pl.multiple_of((3 * cross[g] + i) * UNIT, UNIT), UNIT)
                send_or_copy(
                    weight.at[pl.ds((2 * e + g) * UNIT, UNIT)], wts.at[g, rows],
                    w_as.at[g, e], w_own.at[g], on_ring(g, to, c), to == ring[g],
                )

    def w_sides():
        for g in range(2):
            here = w_block(g, cross[g])
            arrived(here, w_own.at[g])
            for way in range(2):
                send(here, here, w_ss.at[g, way], w_side.at[g, way], cross_to[g][way])

    def w_forward():
        for g in range(2):
            for way in range(2):
                p = wrap(cross[g] + (3, 1)[way])
                arrived(w_block(g, p), w_side.at[g, way])
                half = w_block(g, p, way)
                send(half, half, w_fs.at[g, way], w_d2.at[g], cross_to[g][way])

    def w_far():
        for g in range(2):
            arrived(w_block(g, wrap(cross[g] + 2)), w_d2.at[g])

    def w_left():
        for g in range(2):
            for way in range(2):
                left(w_block(g, 0), w_ss.at[g, way])
                left(w_block(g, 0, 0), w_fs.at[g, way])

    def down_dot(i):
        code_copy(i).wait()
        part = dot(act_v[...], codes_v[i % SLOTS])
        n = i // 2
        if i % 2 == 0:
            d_ps[n] = part.astype(BF)
        else:
            d_own[n] = part
        if i + SLOTS < 8:
            code_copy(i + SLOTS).start()

    def down_share(n):
        send(d_ps.at[n], d_pr.at[n], dp_send.at[n], dp_recv.at[n], partner)

    def down_block(i):
        down_dot(i)
        if i % 2 == 0:
            down_share(i // 2)

    def down_far(h):
        for way in range(2):
            rows = slice(h * HT + way * FT, h * HT + way * FT + FT)
            d_hs[h, way] = (d_own[0, rows] + d_pr[0, rows].astype(F32)).astype(BF)
            send(d_hs.at[h, way], d_hr.at[h, way], dh_send.at[h, way], dh_recv.at[h, way], y_to[way])

    def down_sides(h):
        for way in range(2):
            n = 1 + way
            arrived(d_hr.at[h, way], dh_recv.at[h, way])
            for half in range(2):
                rows = slice(h * HT + half * FT, h * HT + half * FT + FT)
                value = d_own[n, rows] + d_pr[n, rows].astype(F32)
                if half == way:
                    value = value + d_hr[h, way].astype(F32)
                d_bs[h, way, half * FT : half * FT + FT] = value.astype(BF)
            send(d_bs.at[h, way], d_br.at[h, way], db_send.at[h, way], db_recv.at[h, way], y_to[way])

    def down_end(h):
        for way in range(2):
            arrived(d_br.at[h, way], db_recv.at[h, way])
        rows = slice(h * HT, h * HT + HT)
        row_full = jnp.broadcast_to(act_scale[:, rows], (128, HT)).T[:, :1]
        col_full = col_v[...].astype(F32) * QUANT_UNIT
        down = d_own[3, rows] + d_pr[3, rows].astype(F32)
        down = down + d_br[h, 0].astype(F32) + d_br[h, 1].astype(F32)
        high_v[rows] = (res_v[rows].astype(F32) + down * row_full * col_full).astype(BF)
        for q in range(h * NQ // 2, (h + 1) * NQ // 2):
            tap_out(2, q, high_v)

    def down_left():
        for n in range(4):
            left(d_ps.at[n], dp_send.at[n])
        for h in range(2):
            for way in range(2):
                left(d_hs.at[h, way], dh_send.at[h, way])
                left(d_bs.at[h, way], db_send.at[h, way])

    def join_start(q):
        tap_partner(q)
        for g in range(2):
            rows = pl.ds(4 * q * QT, 4 * QT)
            j_s[q, g] = dot(taps[g, rows], wts[g]).astype(BF)
            for r in (2, 1, 3):
                to = wrap(ring[g] + r)
                send(
                    j_s.at[q, g, pl.ds(pl.multiple_of(to * QT, QT), QT)], j_r.at[q, g, r - 1],
                    j_send, j_recv.at[q], on_ring(g, to, c),
                )

    def join_end(q):
        arrived(j_r.at[q], j_recv.at[q])
        rows = slice(q * QT, q * QT + QT)
        joined = jnp.zeros((QT, COL), F32)
        for g in range(2):
            joined = joined + j_s[q, g, pl.ds(pl.multiple_of(ring[g] * QT, QT), QT)].astype(F32)
            for r in range(3):
                joined = joined + j_r[q, g, r].astype(F32)
        j_v[rows] = joined
        grad_norm = go_v[rows].astype(F32) * gain[...]
        lane = lax.broadcasted_iota(jnp.int32, (QT, 128), 1)
        squares = jnp.sum(joined * joined, axis=1, keepdims=True)
        inner = jnp.sum(grad_norm * joined, axis=1, keepdims=True)
        both = jnp.where(lane == 0, squares, jnp.where(lane == 1, inner, 0.0))
        st_s[q] = both.T[:8]
        for r in range(1, 8):
            send(
                st_s.at[q], st_r.at[q, r - 1], st_send, st_recv.at[q],
                {"tensor": lax.rem(t + r, 8), "seq": s},
            )

    def g_piece(g, q, n, r):
        cols = pl.ds(pl.multiple_of((4 * q + r) * QT, QT), QT)
        return gt_v.at[g, pl.ds(n * CW, CW), cols]

    def norm(q):
        arrived(st_r.at[q], st_recv.at[q])
        rows = slice(q * QT, q * QT + QT)
        total = st_s[q]
        for r in range(7):
            total = total + st_r[q, r]
        both = jnp.concatenate([total, jnp.zeros((120, QT), F32)], axis=0).T
        inverse_rms = lax.rsqrt(both[:, 0:1] / D + 1e-05)
        projection = inverse_rms * both[:, 1:2] / D
        normed = j_v[rows] * inverse_rms
        grad_norm = go_v[rows].astype(F32) * gain[...]
        grad_joined = inverse_rms * (grad_norm - normed * projection)
        turned = grad_joined.T.astype(BF)
        for g in range(2):
            gt_v[g, :, pl.ds(pl.multiple_of((4 * q + ring[g]) * QT, QT), QT)] = turned
        for n in range(CHUNKS):
            for g in range(2):
                here = g_piece(g, q, n, ring[g])
                for r in (2, 1, 3):
                    send(
                        here, here, a_send, a_recv.at[g, q, n, r - 1],
                        on_ring(g, wrap(ring[g] + r), c),
                    )
        drafted_v[rows] = (normed * gain[...]).astype(BF)

    def grad_cols(g, p):
        return pl.ds(pl.multiple_of(wrap(cross[g] + p) * XB, XB), XB)

    def grad_early(first, last):
        span = slice(4 * first * QT, 4 * last * QT)
        for n in range(CHUNKS):
            for g in range(2):
                for q in range(first, last):
                    g_wait(g, q, n)

                def add(p, _):
                    part = dot(gt_v[g, n * CW : n * CW + CW, span], taps[g, span, grad_cols(g, p)])
                    if first > 0:
                        part = part + g_own[n, g, p]
                    g_own[n, g, p] = part
                    return 0

                lax.fori_loop(0, 4, add, 0)

    def g_wait(g, q, n):
        for r in range(1, 4):
            arrived(g_piece(g, q, n, wrap(ring[g] - r)), a_recv.at[g, q, n, r - 1])

    def grad_part(g, n, p):
        span = slice(4 * (NQ - 1) * QT, 4 * NQ * QT)
        part = dot(gt_v[g, n * CW : n * CW + CW, span], taps[g, span, grad_cols(g, p)])
        return part + g_own[n, g, p]

    def grad_start(n):
        for g in range(2):
            g_wait(g, NQ - 1, n)
            part = grad_part(g, n, 2).astype(BF)
            for way in range(2):
                g_hs[n, g, way] = part[way * CH : way * CH + CH]
                send(
                    g_hs.at[n, g, way], g_hr.at[n, g, way], gh_send,
                    gh_recv.at[n, g, way], cross_to[g][way],
                )

    def grad_sides(n):
        for g in range(2):
            for way in range(2):
                part = grad_part(g, n, (1, 3)[way])
                arrived(g_hr.at[n, g, way], gh_recv.at[n, g, way])
                for half in range(2):
                    rows = slice(half * CH, half * CH + CH)
                    value = part[rows]
                    if half == way:
                        value = value + g_hr[n, g, way].astype(F32)
                    g_bs[n, g, way, rows] = value.astype(BF)
                send(
                    g_bs.at[n, g, way], g_br.at[n, g, way], gb_send,
                    gb_recv.at[n, g], cross_to[g][way],
                )

    def grad_own(n):
        for g in range(2):
            g_own[n, g, 0] = grad_part(g, n, 0)

    def grad_end(n):
        for g in range(2):
            arrived(g_br.at[n, g], gb_recv.at[n, g])
            total = g_own[n, g, 0] + g_br[n, g, 0].astype(F32) + g_br[n, g, 1].astype(F32)
            f_s[n, g] = total.T.astype(BF)
            for i in range(3):
                if g == 0:
                    q = 4 * i + z
                    to, e = lax.div(q, 3), lax.rem(q, 3)
                else:
                    to, e = wrap(x + z - i), i
                rows = pl.ds(pl.multiple_of((2 * e + g) * UNIT, UNIT), UNIT)
                send_or_copy(
                    f_s.at[n, g, pl.ds(i * UNIT, UNIT)],
                    grad_join.at[rows, pl.ds(n * CW, CW)],
                    f_send.at[n, g, i], f_recv.at[n], on_ring(g, to, c), to == ring[g],
                )

    pl.semaphore_wait(barrier, greeted)
    tap_out(0, 0, tap_low)
    tap_out(1, 0, tap_mid)
    act_copy.wait()
    down_dot(0)
    down_share(0)
    w_out()
    for q in range(1, NQ):
        tap_out(0, q, tap_low)
        tap_out(1, q, tap_mid)

    down_block(1)
    tap_own(0, 0)
    down_block(2)
    arrived(d_pr.at[0], dp_recv.at[0])
    down_far(0)
    down_far(1)
    down_block(3)
    tap_own(1, 0)
    w_sides()
    down_block(4)
    down_block(5)
    for n in (1, 2):
        arrived(d_pr.at[n], dp_recv.at[n])
    down_sides(0)
    down_sides(1)
    tap_own(0, 1)
    tap_sides(0, 0)
    down_block(6)
    tap_sides(1, 0)
    down_block(7)
    tap_own(1, 1)
    w_forward()
    tap_far(0, 0)
    tap_far(1, 0)
    arrived(d_pr.at[3], dp_recv.at[3])
    res_copy.wait()
    col_copy.wait()
    down_end(0)
    tap_sides(0, 1)
    down_end(1)
    tap_own(2, 0)
    tap_sides(1, 1)
    w_far()
    go_copy.wait()
    tap_sides(2, 0)
    tap_own(2, 1)
    tap_far(0, 1)
    tap_far(1, 1)
    tap_own(0, 2)
    tap_far(2, 0)
    join_start(0)
    tap_sides(2, 1)
    tap_own(1, 2)
    tap_own(2, 2)
    tap_far(2, 1)
    join_start(1)
    tap_sides(0, 2)
    join_end(0)
    tap_sides(1, 2)
    tap_own(0, 3)
    tap_sides(2, 2)
    norm(0)
    tap_own(1, 3)
    tap_far(0, 2)
    tap_own(2, 3)
    join_end(1)
    tap_far(1, 2)
    tap_far(2, 2)
    join_start(2)
    tap_sides(0, 3)
    norm(1)
    tap_sides(1, 3)
    tap_sides(2, 3)
    tap_far(0, 3)
    join_end(2)
    tap_far(1, 3)
    tap_far(2, 3)
    join_start(3)
    norm(2)
    drain()
    down_left()
    w_left()
    grad_early(0, 2)
    join_end(3)
    tap_left()
    norm(3)
    grad_early(2, 3)

    drafted_copy = pltpu.make_async_copy(drafted_v, drafted, l_sem.at[4])
    drafted_copy.start()
    for n in range(CHUNKS):
        grad_start(n)
    for n in range(CHUNKS):
        grad_sides(n)
    for n in range(CHUNKS):
        grad_own(n)
        grad_end(n)

    left(j_r, j_send)
    left(st_r, st_send)
    left(taps.at[0, pl.ds(0, 1024)], a_send)
    left(g_hs, gh_send)
    left(g_bs, gb_send)
    drain()
    drafted_copy.wait()
    for n in range(CHUNKS):
        arrived(grad_join.at[:, pl.ds(n * CW, CW)], f_recv.at[n])


def hand_on(drafted, grad_join, drafted_out, grad_join_out):
    drafted_out[...] = drafted[...]
    grad_join_out[...] = grad_join[...]


def on_device(
    tap_low, tap_mid, residual_in, ffn_act, act_scale, down_codes, down_scale,
    join_weight, join_gain, grad_out,
):
    any_ = pl.BlockSpec(memory_space=pl.ANY)
    vmem = pl.BlockSpec(memory_space=pltpu.VMEM)
    V = pltpu.VMEM
    dma = lambda *shape: pltpu.SemaphoreType.DMA(shape)
    one = pltpu.SemaphoreType.DMA
    scratch = [
        V((TOK, HID), BF), V((SLOTS, HID, COL), BF), V((1, COL), jnp.int32),
        V((TOK, COL), BF), V((TOK, COL), BF),
        V((2, 4 * TOK, KG), BF), V((2, KG, COL), BF),
        V((4, TOK, COL), F32), V((4, TOK, COL), BF), V((4, TOK, COL), BF),
        V((2, 2, FT, COL), BF), V((2, 2, FT, COL), BF),
        V((2, 2, HT, COL), BF), V((2, 2, HT, COL), BF),
        V((TOK, COL), BF),
        V((NQ, 2, 4 * QT, COL), BF), V((NQ, 2, 3, QT, COL), BF),
        V((TOK, COL), F32), V((NQ, 8, QT), F32), V((NQ, 7, 8, QT), F32), V((TOK, COL), BF),
        V((2, COL, 4 * TOK), BF), V((CHUNKS, 2, 4, CW, XB), F32),
        V((CHUNKS, 2, 2, CH, XB), BF), V((CHUNKS, 2, 2, CH, XB), BF),
        V((CHUNKS, 2, 2, CW, XB), BF), V((CHUNKS, 2, 2, CW, XB), BF),
        V((CHUNKS, 2, XB, CW), BF),
        dma(5), dma(SLOTS),
        dma(2, 3, NQ), dma(2, 3, NQ, 2), dma(2, 3, NQ), dma(2, NQ),
        dma(2, 3, NQ, 2), dma(2), dma(2), one,
        dma(2), dma(2, 3), dma(2, 2), dma(2), dma(2, 2), dma(2, 2),
        dma(4), dma(4), dma(2, 2), dma(2, 2), dma(2, 2), dma(2, 2),
        dma(NQ), one, dma(NQ), one, dma(2, NQ, CHUNKS, 3), one,
        dma(CHUNKS, 2, 2), one, dma(CHUNKS, 2), one,
        dma(CHUNKS), dma(CHUNKS, 2, 3),
    ]
    shapes = (
        jax.ShapeDtypeStruct((TOK, COL), BF),
        jax.ShapeDtypeStruct((2 * XB, COL), BF),
    )
    results = pl.pallas_call(
        body,
        out_shape=shapes,
        in_specs=[any_, any_, any_, any_, vmem, any_, any_, any_, vmem, any_],
        out_specs=(any_, any_),
        scratch_shapes=scratch,
        compiler_params=pltpu.CompilerParams(
            collective_id=0, has_side_effects=True, vmem_limit_bytes=63 * 1024 * 1024
        ),
        cost_estimate=pl.CostEstimate(
            flops=20_400_000_000, bytes_accessed=30_000_000, transcendentals=0
        ),
        name="tapped_join",
    )(
        tap_low, tap_mid, residual_in, ffn_act, act_scale.reshape(1, TOK), down_codes,
        down_scale.reshape(1, D), join_weight, join_gain.reshape(1, COL), grad_out,
    )
    return pl.pallas_call(
        hand_on,
        out_shape=shapes,
        in_specs=[vmem, vmem],
        out_specs=(vmem, vmem),
        name="hand_on",
    )(*results)


def solution(mesh):
    return jax.shard_map(
        on_device,
        mesh=mesh,
        in_specs=(
            P("seq", "tensor"),
            P("seq", "tensor"),
            P("seq", "tensor"),
            P("seq", "tensor"),
            P("seq"),
            P("tensor", None),
            P(),
            P("seq", "tensor"),
            P("tensor"),
            P("seq", "tensor"),
        ),
        out_specs=(P("seq", "tensor"), P("seq", "tensor")),
        check_vma=False,
    )
```
